128 devices in a mesh: comp: 8 (over x, core), cpl: 16 (over y, z).
Axes of the slice: x: 4, y: 4, z: 4, core: 2. Of those that a mesh axis runs over, the one named last changes fastest.
Arguments:
- atm_fields: bfloat16 [16384, 64, 128], P(('comp', 'cpl')), may hold values from -6 to 6
- land_bits: int32 [16384, 5], P(('comp', 'cpl')), may hold values from 0 to 1073741823
- coupler_owner: int32 [16384], P(('comp', 'cpl')), may hold values from 0 to 127, as said below
- tile_col: int32 [32768], P(('comp', 'cpl')), may hold values from 0 to 255, as said below
- tile_row: int32 [32768], P(('comp', 'cpl')), may hold values from -1 to 511, as said below
- tile_weight: bfloat16 [32768, 4, 128], P(('comp', 'cpl')), may hold values from 0.001953125 to 0.03125
- tile_target: int32 [32768, 4, 128], P(('comp', 'cpl')), may hold values from 0 to 127
Outputs:
- merged: float32 [512, 64, 128], P(('comp', 'cpl'))
The draws below stay inside these ranges and needn't reach their ends.
Inputs may be any that keep to these rules, and one draw needn't show every extreme that they name: `coupler_owner`: of the blocks of one device, at most 2 have one coupler device; in every draw one device receives 2 blocks from every device. `tile_col`: on each device every slot index appears in exactly one tile. `tile_row`: A tile is padding (-1) exactly when its slot is empty. Each ocean block receives exactly 32 tiles, all reading blocks of one atmosphere device; the tiles reading one atmosphere device's blocks add to ocean blocks of one ocean device, a different one for each atmosphere device and never the device itself. So no device holds more than 2 tiles for one ocean device, and in every draw one device holds 2 for every ocean device.
All inputs are finite; a program needn't handle non-finite values.
Results may differ from the reference program's by a relative error of at most 0.00065.
Values may be sent and summed in bfloat16 or wider, within the bound.
No kernel may reach another device: no remote copies, remote signals or barrier semaphores. Data moves between devices by JAX's collectives and lax.ppermute only.
A program may use at most 64 MiB of HBM per device.

```python
import math
import jax
import jax.numpy as jnp
import numpy as np
from jax import lax

FIELDS = 64
BLOCK = 128
ENTRIES = 4
RATIO = 32
OB_DEV = 4
AB_DEV = 128
RANKS = 128
CAP = 2
SLOTS = 256
TILE_CAP = 256
MWORDS = 5
A_BLOCKS = 16384
O_BLOCKS = 512


def owner_table(seed_key):
    hottest = jax.random.randint(jax.random.fold_in(seed_key, 11), (), 0, RANKS)
    others = jnp.arange(RANKS - 1, dtype=jnp.int32)
    others = others + (others >= hottest).astype(jnp.int32)
    tickets = jnp.repeat(others, CAP)

    def one_source(source):
        first_key, second_key = jax.random.split(jax.random.fold_in(seed_key, 100 + source))
        chosen = jax.random.permutation(first_key, tickets)[:AB_DEV - CAP]
        whole = jnp.concatenate([jnp.full((CAP,), hottest, jnp.int32), chosen])
        return jax.random.permutation(second_key, whole)
    return jax.vmap(one_source)(jnp.arange(RANKS, dtype=jnp.int32)).astype(jnp.int32)


def tile_tables(seed_key):
    owners = owner_table(seed_key)
    onehot = (owners[:, :, None] == jnp.arange(RANKS, dtype=jnp.int32)[None, None, :]).astype(jnp.int32)
    rank_in = jnp.sum(jnp.cumsum(onehot, 1) * onehot, 2) - 1
    source = jnp.arange(RANKS, dtype=jnp.int32)[:, None]
    slot_index = source * CAP + rank_in
    order = jax.random.permutation(jax.random.fold_in(seed_key, 17), RANKS).astype(jnp.int32)
    ocean_device = jnp.zeros((RANKS,), jnp.int32).at[order].set(jnp.roll(order, -1))

    def local_blocks(device):
        shuffled = jax.random.permutation(jax.random.fold_in(seed_key, 300 + device), AB_DEV).astype(jnp.int32)
        return shuffled // RATIO
    local = jax.vmap(local_blocks)(jnp.arange(RANKS, dtype=jnp.int32))
    row = ocean_device[:, None] * OB_DEV + local
    row_at = jnp.full((RANKS, SLOTS), -1, jnp.int32).at[owners, slot_index].set(row)

    def per_device(device):
        shuffle = jax.random.permutation(jax.random.fold_in(seed_key, 5000 + device), TILE_CAP).astype(jnp.int32)
        return (shuffle, row_at[device, shuffle])
    columns, ocean_rows = jax.vmap(per_device)(jnp.arange(RANKS, dtype=jnp.int32))
    return (columns.reshape(-1), ocean_rows.reshape(-1))


def draw_coupler_owner(key, part):
    owners = owner_table(key)
    return owners.reshape(-1)


def draw_tile_col(key, part):
    columns, ocean_rows = tile_tables(key)
    return columns


def draw_tile_row(key, part):
    columns, ocean_rows = tile_tables(key)
    return ocean_rows


def touch_ends(values, stream_key, smallest, high):
    spot = [jax.random.randint(jax.random.fold_in(stream_key, axis), (), 0, length) for axis, length in enumerate(values.shape)]
    widest = values.shape.index(max(values.shape))
    next_to = spot[:widest] + [(spot[widest] + 1) % values.shape[widest]] + spot[widest + 1:]
    return values.at[tuple(spot)].set(smallest).at[tuple(next_to)].set(high)


def shard_levels(rng, extent, cuts, least, high):
    factor_of, own = 1.0, jax.random.fold_in(rng, 6)
    for axis_at, parts in cuts:
        draws = jnp.exp(jax.random.uniform(jax.random.fold_in(own, axis_at), (parts,), jnp.float32, least / len(cuts), high / len(cuts)))
        factor_of = factor_of * jnp.repeat(draws, extent[axis_at] // parts).reshape([-1 if axis == axis_at else 1 for axis in range(len(extent))])
    return factor_of


def centred(own_key, extent, deviation, most, cuts=(), kind=jnp.bfloat16):
    loudness = shard_levels(own_key, extent, cuts, -0.22, 0.18) if cuts else 1.0
    values = jax.random.normal(own_key, extent, jnp.float32) * deviation * loudness
    return jnp.minimum(jnp.maximum(values, -most), most).astype(kind)


def setup_inputs(seed: int = 0) -> dict:
    seeds = jax.random.split(jax.random.key(seed), 8)
    atm_fields = centred(seeds[0], (A_BLOCKS, FIELDS, BLOCK), 1.0, 6.0, ((0, 128),))
    land_bits = touch_ends(jax.random.randint(seeds[1], (A_BLOCKS, MWORDS), 0, 1073741824), jax.random.fold_in(seeds[1], 1), 0, 1073741823).astype(jnp.int32)
    coupler_owner = draw_coupler_owner(jax.random.fold_in(seeds[7], 71), 0)
    tile_col = draw_tile_col(jax.random.fold_in(seeds[7], 71), 0)
    tile_row = draw_tile_row(jax.random.fold_in(seeds[7], 71), 0)
    tile_weight = jnp.clip(jnp.exp(math.log(0.03125) - 2.7725887 * jax.random.uniform(seeds[5], (RANKS * TILE_CAP, ENTRIES, BLOCK), jnp.float32) ** shard_levels(seeds[5], (RANKS * TILE_CAP, ENTRIES, BLOCK), ((0, 128),), -0.2, 0.2)), 0.001953125, 0.03125).astype(jnp.bfloat16)
    tile_target = touch_ends(jax.random.randint(seeds[6], (RANKS * TILE_CAP, ENTRIES, BLOCK), 0, BLOCK), jax.random.fold_in(seeds[6], 1), 0, BLOCK - 1).astype(jnp.int32)
    return dict(atm_fields=atm_fields, land_bits=land_bits, coupler_owner=coupler_owner, tile_col=tile_col, tile_row=tile_row, tile_weight=tile_weight, tile_target=tile_target)


drag_coef = 0.5
heat_coef = 0.5
vapor_coef = 0.5

def surface_fluxes(state_fields, packed_bits):
    columns = np.arange(state_fields.shape[2])
    packed = packed_bits[:, columns // 30]
    ocean = jnp.right_shift(packed, jnp.asarray(columns % 30, dtype=jnp.int32)) & 1 == 1
    state = state_fields[:, :6].astype(jnp.float32)
    wind_east = state[:, 0]
    wind_north = state[:, 1]
    wind_speed = jnp.sqrt(wind_east * wind_east + wind_north * wind_north + 0.25)
    bulk = jnp.stack([drag_coef * wind_speed * wind_east, drag_coef * wind_speed * wind_north, heat_coef * wind_speed * (state[:, 4] - state[:, 2]), vapor_coef * wind_speed * (state[:, 5] - state[:, 3])], 1)
    blended = jnp.where(ocean[:, None, :], bulk, state[:, :4]).astype(jnp.bfloat16)
    return jnp.concatenate([blended, state_fields[:, 4:]], 1)

def one_tile(block_fluxes, weight, target):
    products = (block_fluxes[:, None, :] * weight[None, :, :]).reshape(FIELDS, ENTRIES * BLOCK)
    return jnp.zeros((FIELDS, BLOCK), jnp.float32).at[:, target.reshape(-1)].add(products)

def reference(atm_fields, land_bits, coupler_owner, tile_col, tile_row, tile_weight, tile_target):
    fluxes = surface_fluxes(atm_fields, land_bits)
    owners = coupler_owner.reshape(RANKS, AB_DEV)
    onehot = (owners[:, :, None] == jnp.arange(RANKS, dtype=jnp.int32)[None, None, :]).astype(jnp.int32)
    rank_in = lax.optimization_barrier(jnp.sum(jnp.cumsum(onehot, 1) * onehot, 2)) - 1
    source = jnp.arange(RANKS, dtype=jnp.int32)[:, None]
    global_ids = source * AB_DEV + jnp.arange(AB_DEV, dtype=jnp.int32)[None, :]
    slot_block = jnp.zeros((RANKS, SLOTS), jnp.int32).at[owners, source * CAP + rank_in].set(global_ids)
    columns = tile_col.reshape(RANKS, TILE_CAP)
    ocean_rows = tile_row.reshape(RANKS, TILE_CAP)
    weights = tile_weight.reshape(RANKS, TILE_CAP, ENTRIES, BLOCK)
    targets = tile_target.reshape(RANKS, TILE_CAP, ENTRIES, BLOCK)

    def accumulate(running, inputs):
        slot_row, column, ocean_row, weight, target = inputs
        block_ids = slot_row[column]
        picked = fluxes[block_ids].astype(jnp.float32)
        partial_value = jax.vmap(one_tile)(picked, weight.astype(jnp.float32), target)
        segment = jnp.where(ocean_row >= 0, ocean_row, O_BLOCKS)
        added = jax.ops.segment_sum(partial_value, segment, num_segments=O_BLOCKS + 1)[:O_BLOCKS]
        return (running + added, None)
    merged, unused = lax.scan(accumulate, jnp.zeros((O_BLOCKS, FIELDS, BLOCK), jnp.float32), (slot_block, columns, ocean_rows, weights, targets))
    return merged
```

```python
import jax
import jax.numpy as jnp
from jax import lax
from jax.experimental import pallas as pl
from jax.experimental.pallas import tpu as pltpu
from jax.sharding import PartitionSpec as P

AXES = ("comp", "cpl")
ENTRIES = 4
CHUNK = 5
VMEM_LIMIT = 24 * 1024 * 1024


def pack_kernel(ranks, ocean_blocks, col_ref, row_ref, weight_ref, target_ref, out_ref, slot_row):
    tiles = weight_ref.shape[0]
    block = weight_ref.shape[2]

    def place(t, carry):
        slot = col_ref[t]
        slot_row[slot] = row_ref[t]
        base = (slot >> 1) * CHUNK + (slot & 1) * 2
        out_ref[base] = weight_ref[t]
        out_ref[base + 1] = target_ref[t].astype(jnp.float32).astype(jnp.bfloat16)
        return carry

    lax.fori_loop(0, tiles, place, 0, unroll=8)

    lane = lax.broadcasted_iota(jnp.int32, (1, block), 1)

    def destination(s, found):
        best = jnp.maximum(slot_row[2 * s], slot_row[2 * s + 1])
        device = jnp.where(best >= 0, best // ocean_blocks + 1, 0)
        return jnp.where(lane == s, device, found)

    found = lax.fori_loop(0, ranks, destination, jnp.zeros((1, block), jnp.int32), unroll=8)
    entry = lax.broadcasted_iota(jnp.int32, (ENTRIES, block), 0)
    found = jnp.where(entry == 2, jnp.broadcast_to(found, (ENTRIES, block)), 0)

    def rows_of(s, carry):
        first = slot_row[2 * s]
        second = slot_row[2 * s + 1]
        first = jnp.where(first >= 0, first % ocean_blocks + 1, 0)
        second = jnp.where(second >= 0, second % ocean_blocks + 1, 0)
        rows = jnp.where(entry == 0, first, jnp.where(entry == 1, second, found))
        out_ref[s * CHUNK + 4] = rows.astype(jnp.float32).astype(jnp.bfloat16)
        return carry

    lax.fori_loop(0, ranks, rows_of, 0, unroll=8)


def flux_kernel(owner_ref, bits_ref, atm_ref, sent_ref, out_ref, slot_ref, ocean_ref, count_ref):
    blocks, _, block = atm_ref.shape

    def clear(c, carry):
        count_ref[c] = 0
        return carry

    lax.fori_loop(0, count_ref.shape[0], clear, 0, unroll=8)

    def home(b, carry):
        owner = owner_ref[b]
        rank = count_ref[owner]
        count_ref[owner] = rank + 1
        slot_ref[b] = 2 * owner + rank
        return carry

    lax.fori_loop(0, blocks, home, 0, unroll=4)

    column = lax.broadcasted_iota(jnp.int32, (blocks, block), 1)
    word = column // 30
    bits = bits_ref[...]
    picked = jnp.zeros((blocks, block), jnp.int32)
    for w in range(bits.shape[1]):
        picked = jnp.where(word == w, jnp.broadcast_to(bits[:, w : w + 1], (blocks, block)), picked)
    ocean_ref[...] = jnp.right_shift(picked, column - word * 30) & 1

    field = lax.broadcasted_iota(jnp.int32, (8, block), 0)

    def one_block(b, carry):
        state = atm_ref[b, 0:16, :].astype(jnp.float32)
        head = state[0:8]
        wind_east = head[0:1]
        wind_north = head[1:2]
        speed = jnp.sqrt(wind_east * wind_east + wind_north * wind_north + 0.25)
        later = pltpu.roll(head, 6, 0)
        drive = jnp.where(field < 2, head, later - head)
        bulk = (0.5 * speed) * drive
        ocean = jnp.broadcast_to(ocean_ref[pl.ds(b, 1), :], (8, block))
        head = jnp.where((ocean == 1) & (field < 4), bulk, head)
        out_ref[b, 0:16, :] = jnp.concatenate([head, state[8:16]], 0).astype(jnp.bfloat16)
        out_ref[b, 16:64, :] = atm_ref[b, 16:64, :]
        return carry

    lax.fori_loop(0, blocks, one_block, 0, unroll=4)


def remap_kernel(slot_ref, recv_ref, flux_ref, out_ref, owner_ref, rows_vmem, rows_smem, sem):
    blocks, _, block = flux_ref.shape
    ranks = recv_ref.shape[0] // CHUNK
    entry = lax.broadcasted_iota(jnp.int32, (ENTRIES, block), 0)
    lane = lax.broadcasted_iota(jnp.int32, (ENTRIES, block), 1)

    def gather_rows(c, found):
        rows = recv_ref[c * CHUNK + 4].astype(jnp.float32)
        return jnp.maximum(found, jnp.where((lane == c) | (entry == 2), rows, 0.0))

    found = lax.fori_loop(0, ranks, gather_rows, jnp.zeros((ENTRIES, block), jnp.float32), unroll=8)
    found = jnp.concatenate([found, jnp.zeros((ENTRIES, block), jnp.float32)], 0)
    owner_ref[...] = found
    rows_vmem[...] = found.astype(jnp.int32)
    copy = pltpu.make_async_copy(rows_vmem, rows_smem, sem)
    copy.start()
    out_ref[...] = jnp.zeros_like(out_ref)
    copy.wait()

    column = lax.broadcasted_iota(jnp.int32, (block, block), 0).astype(jnp.float32).astype(jnp.bfloat16)

    def one_tile(b, carry):
        slot = slot_ref[b]
        source = slot >> 1
        rank = slot & 1
        base = source * CHUNK + rank * 2
        row = rows_smem[rank, source] - 1
        weight = recv_ref[base]
        target = recv_ref[base + 1]
        dense = [
            jnp.where(
                jnp.broadcast_to(target[k : k + 1], (block, block)) == column,
                jnp.broadcast_to(weight[k : k + 1], (block, block)),
                jnp.zeros((), jnp.bfloat16),
            )
            for k in range(ENTRIES)
        ]
        fluxes = flux_ref[b]
        out_ref[row] += lax.dot_general(
            jnp.concatenate([fluxes] * ENTRIES, 1),
            jnp.concatenate(dense, 1),
            (((1,), (1,)), ((), ())),
            preferred_element_type=jnp.float32,
        )
        return carry

    lax.fori_loop(0, blocks, one_tile, 0, unroll=4)


def permute_kernel(owner_ref, x_ref, out_ref):
    ranks, pieces, block = x_ref.shape
    rows = ranks * pieces
    source = lax.broadcasted_iota(jnp.int32, (block, rows), 0)
    spread = (lax.broadcasted_iota(jnp.int32, (block, rows), 1) // pieces == source)
    owner = jnp.dot(
        owner_ref[...].astype(jnp.bfloat16),
        spread.astype(jnp.float32).astype(jnp.bfloat16),
        preferred_element_type=jnp.float32,
    )[2:3]
    half = lax.broadcasted_iota(jnp.int32, (1, rows), 1) % pieces
    wanted = (owner.astype(jnp.int32) - 1) * pieces + half
    chosen = lax.broadcasted_iota(jnp.int32, (rows, rows), 0) == jnp.broadcast_to(wanted, (rows, rows))
    chosen = chosen.astype(jnp.float32).astype(jnp.bfloat16)
    value = x_ref[...].reshape(rows, block)
    high = value.astype(jnp.bfloat16)
    rest = value - high.astype(jnp.float32)
    middle = rest.astype(jnp.bfloat16)
    low = (rest - middle.astype(jnp.float32)).astype(jnp.bfloat16)
    total = jnp.dot(chosen, high, preferred_element_type=jnp.float32)
    total += jnp.dot(chosen, middle, preferred_element_type=jnp.float32)
    total += jnp.dot(chosen, low, preferred_element_type=jnp.float32)
    out_ref[...] = total.reshape(ranks, pieces, block)


def smem():
    return pl.BlockSpec(memory_space=pltpu.SMEM)


def vmem():
    return pl.BlockSpec(memory_space=pltpu.VMEM)


def exchange(x):
    return lax.all_to_all(x, AXES, split_axis=0, concat_axis=0, tiled=True)


def on_device(atm_fields, land_bits, coupler_owner, tile_col, tile_row, tile_weight, tile_target):
    ranks = lax.axis_size("comp") * lax.axis_size("cpl")
    blocks, fields, block = atm_fields.shape
    ocean_blocks = blocks // 32
    params = pltpu.CompilerParams(vmem_limit_bytes=VMEM_LIMIT)

    send = pl.pallas_call(
        lambda *refs: pack_kernel(ranks, ocean_blocks, *refs),
        out_shape=jax.ShapeDtypeStruct((ranks * CHUNK, ENTRIES, block), jnp.bfloat16),
        in_specs=[smem(), smem(), vmem(), vmem()],
        out_specs=vmem(),
        scratch_shapes=[pltpu.SMEM((tile_col.shape[0],), jnp.int32)],
        compiler_params=params,
        name="pack",
    )(tile_col, tile_row, tile_weight, tile_target)
    recv = exchange(send)

    fluxes, slot = pl.pallas_call(
        flux_kernel,
        out_shape=(
            jax.ShapeDtypeStruct(atm_fields.shape, jnp.bfloat16),
            jax.ShapeDtypeStruct((blocks,), jnp.int32),
        ),
        in_specs=[smem(), vmem(), vmem(), pl.BlockSpec(memory_space=pl.ANY)],
        out_specs=(vmem(), smem()),
        scratch_shapes=[pltpu.VMEM((blocks, block), jnp.int32), pltpu.SMEM((ranks,), jnp.int32)],
        compiler_params=params,
        cost_estimate=pl.CostEstimate(flops=10_000_000, bytes_accessed=4_000_000, transcendentals=0),
        name="flux",
    )(coupler_owner, land_bits, atm_fields, send)

    sums, owner = pl.pallas_call(
        remap_kernel,
        out_shape=(
            jax.ShapeDtypeStruct((ocean_blocks, fields, block), jnp.float32),
            jax.ShapeDtypeStruct((8, block), jnp.float32),
        ),
        in_specs=[smem(), vmem(), vmem()],
        out_specs=(vmem(), vmem()),
        scratch_shapes=[
            pltpu.VMEM((8, block), jnp.int32),
            pltpu.SMEM((8, block), jnp.int32),
            pltpu.SemaphoreType.DMA,
        ],
        compiler_params=params,
        name="remap",
    )(slot, recv, fluxes)

    pieces = ocean_blocks * fields // ranks
    spread = exchange(sums.reshape(ranks, pieces, block))
    turned = pl.pallas_call(
        permute_kernel,
        out_shape=jax.ShapeDtypeStruct(spread.shape, jnp.float32),
        in_specs=[vmem(), vmem()],
        out_specs=vmem(),
        compiler_params=params,
        name="permute",
    )(owner, spread)
    return exchange(turned).reshape(ocean_blocks, fields, block)


def solution(mesh):
    in_specs = (
        P(AXES, None, None),
        P(AXES, None),
        P(AXES),
        P(AXES),
        P(AXES),
        P(AXES, None, None),
        P(AXES, None, None),
    )
    return jax.shard_map(
        on_device, mesh=mesh, in_specs=in_specs, out_specs=P(AXES, None, None), check_vma=False
    )
```

```python
import jax
import jax.numpy as jnp
from jax import lax
from jax.experimental import pallas as pl
from jax.experimental.pallas import tpu as pltpu
from jax.sharding import PartitionSpec as P

AXES = ("comp", "cpl")
ENTRIES = 4
RATIO = 32
CHUNK = 5
VMEM_LIMIT = 24 * 1024 * 1024
BF16 = jnp.bfloat16
F32 = jnp.float32
I32 = jnp.int32
ROWS_WITH_ROWS = (((1,), (1,)), ((), ()))


def start_copies(pairs, sems):
    copies = [pltpu.make_async_copy(a, b, sems.at[i]) for i, (a, b) in enumerate(pairs)]
    for copy in copies:
        copy.start()
    return copies


def regroup(target, weight):
    t0, t1, t2, t3 = target
    w0, w1, w2, w3 = weight
    e01, e02, e03 = t0 == t1, t0 == t2, t0 == t3
    e12, e13, e23 = t1 == t2, t1 == t3, t2 == t3
    zero = jnp.zeros_like(w0)
    swap = e01 | e23
    a1t, a1w = jnp.where(swap, t2, t1), jnp.where(swap, w2, w1)
    b0t, b0w = jnp.where(swap, t1, t2), jnp.where(swap, w1, w2)
    with_first = (e01 & e02) | (e01 & e03) | (e02 & e03)
    rest = e12 & e13 & jnp.logical_not(with_first)
    sum0 = w0 + jnp.where(e01, w1, zero) + jnp.where(e02, w2, zero) + jnp.where(e03, w3, zero)
    sum1 = w1 + w2 + w3
    high0 = sum0.astype(BF16).astype(F32)
    high1 = sum1.astype(BF16).astype(F32)
    other_t = jnp.where(e01, jnp.where(e02, t3, t2), t1)
    other_w = jnp.where(e01, jnp.where(e02, w3, w2), w1)
    a0w = jnp.where(with_first, high0, w0)
    a1t = jnp.where(with_first, other_t, jnp.where(rest, t1, a1t))
    a1w = jnp.where(with_first, other_w, jnp.where(rest, high1, a1w))
    b0t = jnp.where(with_first, t0, jnp.where(rest, t1, b0t))
    b0w = jnp.where(with_first, sum0 - high0, jnp.where(rest, sum1 - high1, b0w))
    b1t = jnp.where(with_first, t0, jnp.where(rest, t1, t3))
    b1w = jnp.where(with_first | rest, b0w, w3)
    return (t0, a1t, b0t, b1t), (a0w, a1w, b0w, b1w)


def pack_kernel(
    ranks, ocean_blocks, col_hbm, col2_hbm, row2_hbm, weight_hbm, target_hbm,
    out_ref, col, col2, row2, weight_in, target_in, weight, target, sems,
):
    tiles = col.shape[0]
    block = weight.shape[1]
    halves = tiles // block
    copies = start_copies(
        ((col2_hbm, col2), (row2_hbm, row2), (col_hbm, col), (weight_hbm, weight_in), (target_hbm, target_in)), sems
    )

    copies[0].wait()
    copies[1].wait()
    slot = (col2[...] & 1) * ranks + (col2[...] >> 1)
    entry = lax.broadcasted_iota(I32, (8, block), 0)
    place = lax.broadcasted_iota(I32, (tiles, block), 0)
    onehot, values = [], []
    for h in range(halves):
        same = jnp.broadcast_to(slot[h : h + 1], (tiles, block)) == place
        onehot.append(jnp.where(same, 1.0, 0.0).astype(BF16))
        row = jnp.broadcast_to(row2[h : h + 1], (8, block))
        device = jnp.where(row >= 0, row // ocean_blocks + 1, 0)
        local = jnp.where(row >= 0, row % ocean_blocks, 0)
        values.append(jnp.where(entry == 0, local, device).astype(F32).astype(BF16))
    found = lax.dot_general(
        jnp.concatenate(values, 1), jnp.concatenate(onehot, 1), ROWS_WITH_ROWS, preferred_element_type=F32
    )
    entry = entry[:ENTRIES]
    local0 = jnp.broadcast_to(found[0:1, :ranks], (ENTRIES, block))
    local1 = jnp.broadcast_to(found[0:1, ranks:], (ENTRIES, block))
    device = jnp.broadcast_to(jnp.maximum(found[1:2, :ranks], found[1:2, ranks:]), (ENTRIES, block))
    info = jnp.where(entry == 0, local0, jnp.where(entry == 1, local1, device)).astype(BF16)

    def tell(s, carry):
        out_ref[s * CHUNK + 4] = info
        return carry

    lax.fori_loop(0, ranks, tell, 0, unroll=16)

    copies[3].wait()

    def widen(g, carry):
        at = pl.ds(pl.multiple_of(g * 16, 16), 16)
        weight[at] = weight_in[at].astype(F32)
        return carry

    lax.fori_loop(0, weight.shape[0] // 16, widen, 0, unroll=8)
    copies[4].wait()

    def pair_up(g, carry):
        base = pl.multiple_of(g * 32, 32)
        at = [pl.ds(base + k, 8, ENTRIES) for k in range(ENTRIES)]
        targets, weights = regroup([target_in[a, :] for a in at], [weight[a, :] for a in at])
        for k in range(ENTRIES):
            target[at[k], :] = targets[k].astype(F32)
            weight[at[k], :] = weights[k]
        return carry

    lax.fori_loop(0, weight.shape[0] // 32, pair_up, 0, unroll=4)
    copies[2].wait()

    def send(t, carry):
        home = col[t]
        base = (home >> 1) * CHUNK + (home & 1) * 2
        at = pl.ds(pl.multiple_of(t * ENTRIES, ENTRIES), ENTRIES)
        out_ref[base] = weight[at, :].astype(BF16)
        out_ref[base + 1] = target[at, :].astype(BF16)
        return carry

    lax.fori_loop(0, tiles, send, 0, unroll=16)


def flux_kernel(
    owner_hbm, bits_hbm, atm_hbm, sent_hbm, out_hbm, slot_hbm,
    owner, slot, count, bits, atm, out, ocean, sems,
):
    blocks, fields, block = atm.shape
    words = bits.shape[0]
    copies = start_copies(((owner_hbm, owner), (bits_hbm, bits), (atm_hbm, atm)), sems)

    def clear(c, carry):
        count[c] = 0
        return carry

    lax.fori_loop(0, count.shape[0], clear, 0, unroll=16)
    copies[0].wait()

    def home(b, carry):
        to = owner[b]
        rank = count[to]
        count[to] = rank + 1
        slot[b] = 2 * to + rank
        return carry

    lax.fori_loop(0, blocks, home, 0, unroll=8)
    slots_out = pltpu.make_async_copy(slot, slot_hbm, sems.at[3])
    slots_out.start()

    copies[1].wait()
    column = lax.broadcasted_iota(I32, (blocks, block), 1)
    word = column // 30
    packed = jnp.concatenate([bits[...], jnp.zeros((8 - words, blocks), I32)], 0).T
    picked = jnp.zeros((blocks, block), I32)
    for w in range(words):
        picked = jnp.where(word == w, jnp.broadcast_to(packed[:, w : w + 1], (blocks, block)), picked)
    ocean[...] = jnp.right_shift(picked, column - word * 30) & 1

    copies[2].wait()
    field = lax.broadcasted_iota(I32, (8, block), 0)

    def fluxes_of(b):
        state = atm[b, 0:16, :].astype(F32)
        head = state[0:8]
        wind_east = head[0:1]
        wind_north = head[1:2]
        speed = jnp.sqrt(wind_east * wind_east + wind_north * wind_north + 0.25)
        drive = jnp.where(field < 2, head, pltpu.roll(head, 6, 0) - head)
        is_ocean = jnp.broadcast_to(ocean[pl.ds(b, 1), :], (8, block)) == 1
        head = jnp.where(is_ocean & (field < 4), (0.5 * speed) * drive, head)
        return jnp.concatenate([jnp.concatenate([head, state[8:16]], 0).astype(BF16), atm[b, 16:fields, :]], 0)

    def pair(p, carry):
        out[p] = jnp.concatenate([fluxes_of(2 * p), fluxes_of(2 * p + 1)], 0).T
        return carry

    lax.fori_loop(0, blocks // 2, pair, 0, unroll=4)
    fluxes_out = pltpu.make_async_copy(out, out_hbm, sems.at[4])
    fluxes_out.start()
    fluxes_out.wait()
    slots_out.wait()


def remap_kernel(
    ranks, slot_hbm, recv, flux_hbm, out_ref, owner_ref,
    slot, flux, sum_even, sum_odd, rows_vmem, rows, sems,
):
    pairs, block, _ = flux.shape
    fields = out_ref.shape[1]
    copies = start_copies(((slot_hbm, slot), (flux_hbm, flux)), sems)
    me = lax.axis_index("comp") * lax.axis_size("cpl") + lax.axis_index("cpl")
    entry_lane = lax.broadcasted_iota(I32, (ENTRIES, block), 1)

    def hear(c, carry):
        mine, device = carry
        info = recv[c * CHUNK + 4].astype(F32)
        moved = pltpu.roll(info, lax.rem(c - me + ranks, ranks), 1)
        return jnp.maximum(mine, jnp.where(entry_lane == c, moved, 0.0)), jnp.maximum(device, info)

    zeros = jnp.zeros((ENTRIES, block), F32)
    mine, device = lax.fori_loop(0, ranks, hear, (zeros, zeros), unroll=16)
    rows_vmem[...] = jnp.concatenate([mine, zeros], 0).astype(I32)
    rows_in = pltpu.make_async_copy(rows_vmem, rows, sems.at[2])
    rows_in.start()
    owner_ref[...] = jnp.concatenate([device, zeros], 0)
    sum_even[...] = jnp.zeros_like(sum_even)
    sum_odd[...] = jnp.zeros_like(sum_odd)
    column = lax.broadcasted_iota(I32, (block, block), 0).astype(F32).astype(BF16)
    nothing = jnp.zeros((), BF16)

    def spread(x):
        return jnp.broadcast_to(x, (block, block))

    def dense(b):
        home = slot[b]
        base = (home >> 1) * CHUNK + (home & 1) * 2
        weight = recv[base]
        target = recv[base + 1]

        def two(k):
            second = jnp.where(spread(target[k + 1 : k + 2]) == column, spread(weight[k + 1 : k + 2]), nothing)
            return jnp.where(spread(target[k : k + 1]) == column, spread(weight[k : k + 1]), second)

        return rows[home & 1, home >> 1], jnp.concatenate([two(0), two(2)], 1)

    def pair(p, carry):
        row0, dense0 = dense(2 * p)
        row1, dense1 = dense(2 * p + 1)
        both = flux[p]
        terms = jnp.dot(
            jnp.concatenate([dense0, dense1], 0), jnp.concatenate([both, both], 0), preferred_element_type=F32
        )
        sum_even[row0] += terms[:block]
        sum_odd[row1] += terms[block:]
        return carry

    for copy in copies:
        copy.wait()
    rows_in.wait()
    lax.fori_loop(0, pairs, pair, 0, unroll=pairs)
    for q in range(out_ref.shape[0]):
        total = sum_even[q] + pltpu.roll(sum_odd[q], fields, 1)
        out_ref[q] = total.T[:fields]


def permute_kernel(owner_ref, x_ref, out_ref):
    ranks, pieces, block = x_ref.shape
    rows = ranks * pieces
    source = lax.broadcasted_iota(I32, (block, rows), 0)
    spread = lax.broadcasted_iota(I32, (block, rows), 1) // pieces == source
    owner = jnp.dot(
        owner_ref[...].astype(BF16), spread.astype(F32).astype(BF16), preferred_element_type=F32
    )[2:3]
    half = lax.broadcasted_iota(I32, (1, rows), 1) % pieces
    wanted = (owner.astype(I32) - 1) * pieces + half
    chosen = lax.broadcasted_iota(I32, (rows, rows), 0) == jnp.broadcast_to(wanted, (rows, rows))
    chosen = chosen.astype(F32).astype(BF16)
    value = x_ref[...].reshape(rows, block)
    high = value.astype(BF16)
    left = value - high.astype(F32)
    middle = left.astype(BF16)
    low = (left - middle.astype(F32)).astype(BF16)
    total = jnp.dot(chosen, high, preferred_element_type=F32)
    total += jnp.dot(chosen, middle, preferred_element_type=F32)
    total += jnp.dot(chosen, low, preferred_element_type=F32)
    out_ref[...] = total.reshape(ranks, pieces, block)


def hbm():
    return pl.BlockSpec(memory_space=pltpu.HBM)


def vmem():
    return pl.BlockSpec(memory_space=pltpu.VMEM)


def in_hbm(x):
    return pltpu.with_memory_space_constraint(x, pltpu.HBM)


def exchange(x):
    return lax.all_to_all(x, AXES, split_axis=0, concat_axis=0, tiled=True)


def on_device(atm_fields, land_bits, coupler_owner, tile_col, tile_row, tile_weight, tile_target):
    ranks = lax.axis_size("comp") * lax.axis_size("cpl")
    blocks, fields, block = atm_fields.shape
    words = land_bits.shape[1]
    tiles = tile_col.shape[0]
    lines = tiles * ENTRIES
    ocean_blocks = blocks // RATIO
    params = pltpu.CompilerParams(vmem_limit_bytes=VMEM_LIMIT)

    send = pl.pallas_call(
        lambda *refs: pack_kernel(ranks, ocean_blocks, *refs),
        out_shape=jax.ShapeDtypeStruct((ranks * CHUNK, ENTRIES, block), BF16),
        in_specs=[hbm()] * 5,
        out_specs=vmem(),
        scratch_shapes=[
            pltpu.SMEM((tiles,), I32),
            pltpu.VMEM((tiles // block, block), I32),
            pltpu.VMEM((tiles // block, block), I32),
            pltpu.VMEM((lines, block), BF16),
            pltpu.VMEM((lines, block), I32),
            pltpu.VMEM((lines, block), F32),
            pltpu.VMEM((lines, block), F32),
            pltpu.SemaphoreType.DMA((5,)),
        ],
        compiler_params=params,
        name="pack",
    )(
        in_hbm(tile_col),
        in_hbm(tile_col.reshape(tiles // block, block)),
        in_hbm(tile_row.reshape(tiles // block, block)),
        in_hbm(tile_weight.reshape(lines, block)),
        in_hbm(tile_target.reshape(lines, block)),
    )
    recv = exchange(send)

    fluxes, slot = pl.pallas_call(
        flux_kernel,
        out_shape=(pltpu.HBM((blocks // 2, block, 2 * fields), BF16), pltpu.HBM((blocks,), I32)),
        in_specs=[hbm()] * 3 + [pl.BlockSpec(memory_space=pl.ANY)],
        out_specs=(hbm(), hbm()),
        scratch_shapes=[
            pltpu.SMEM((blocks,), I32),
            pltpu.SMEM((blocks,), I32),
            pltpu.SMEM((ranks,), I32),
            pltpu.VMEM((words, blocks), I32),
            pltpu.VMEM((blocks, fields, block), BF16),
            pltpu.VMEM((blocks // 2, block, 2 * fields), BF16),
            pltpu.VMEM((blocks, block), I32),
            pltpu.SemaphoreType.DMA((5,)),
        ],
        compiler_params=params,
        cost_estimate=pl.CostEstimate(flops=10_000_000, bytes_accessed=4_000_000, transcendentals=0),
        name="flux",
    )(in_hbm(coupler_owner), in_hbm(land_bits.T), in_hbm(atm_fields), send)

    sums, owner = pl.pallas_call(
        lambda *refs: remap_kernel(ranks, *refs),
        out_shape=(
            jax.ShapeDtypeStruct((ocean_blocks, fields, block), F32),
            jax.ShapeDtypeStruct((8, block), F32),
        ),
        in_specs=[hbm(), vmem(), hbm()],
        out_specs=(vmem(), vmem()),
        scratch_shapes=[
            pltpu.SMEM((blocks,), I32),
            pltpu.VMEM((blocks // 2, block, 2 * fields), BF16),
            pltpu.VMEM((ocean_blocks, block, 2 * fields), F32),
            pltpu.VMEM((ocean_blocks, block, 2 * fields), F32),
            pltpu.VMEM((8, block), I32),
            pltpu.SMEM((8, block), I32),
            pltpu.SemaphoreType.DMA((3,)),
        ],
        compiler_params=params,
        name="remap",
    )(in_hbm(slot), recv, in_hbm(fluxes))

    pieces = ocean_blocks * fields // ranks
    spread = exchange(sums.reshape(ranks, pieces, block))
    turned = pl.pallas_call(
        permute_kernel,
        out_shape=jax.ShapeDtypeStruct(spread.shape, F32),
        in_specs=[vmem(), vmem()],
        out_specs=vmem(),
        compiler_params=params,
        name="permute",
    )(owner, spread)
    return exchange(turned).reshape(ocean_blocks, fields, block)


def solution(mesh):
    in_specs = (
        P(AXES, None, None),
        P(AXES, None),
        P(AXES),
        P(AXES),
        P(AXES),
        P(AXES, None, None),
        P(AXES, None, None),
    )
    return jax.shard_map(
        on_device, mesh=mesh, in_specs=in_specs, out_specs=P(AXES, None, None), check_vma=False
    )
```

```python
import jax
import jax.numpy as jnp
from jax import lax
from jax.experimental import pallas as pl
from jax.experimental.pallas import tpu as pltpu
from jax.sharding import PartitionSpec as P

AXES = ("comp", "cpl")
ENTRIES = 4
RATIO = 32
CHUNK = 9
TILE_PAIRS = 4
STAGES = 4
VMEM_LIMIT = 24 * 1024 * 1024
BF16 = jnp.bfloat16
F32 = jnp.float32
I32 = jnp.int32
ROWS_WITH_ROWS = (((1,), (1,)), ((), ()))


def start_copies(pairs, sems):
    copies = [pltpu.make_async_copy(a, b, sems.at[i]) for i, (a, b) in enumerate(pairs)]
    for copy in copies:
        copy.start()
    return copies


def regroup(target, weight):
    t0, t1, t2, t3 = target
    w0, w1, w2, w3 = weight
    e01, e02, e03 = t0 == t1, t0 == t2, t0 == t3
    e12, e13, e23 = t1 == t2, t1 == t3, t2 == t3
    zero = jnp.zeros_like(w0)
    swap = e01 | e23
    a1t, a1w = jnp.where(swap, t2, t1), jnp.where(swap, w2, w1)
    b0t, b0w = jnp.where(swap, t1, t2), jnp.where(swap, w1, w2)
    with_first = (e01 & e02) | (e01 & e03) | (e02 & e03)
    rest = e12 & e13 & jnp.logical_not(with_first)
    sum0 = w0 + jnp.where(e01, w1, zero) + jnp.where(e02, w2, zero) + jnp.where(e03, w3, zero)
    sum1 = w1 + w2 + w3
    high0 = sum0.astype(BF16).astype(F32)
    high1 = sum1.astype(BF16).astype(F32)
    other_t = jnp.where(e01, jnp.where(e02, t3, t2), t1)
    other_w = jnp.where(e01, jnp.where(e02, w3, w2), w1)
    a0w = jnp.where(with_first, high0, w0)
    a1t = jnp.where(with_first, other_t, jnp.where(rest, t1, a1t))
    a1w = jnp.where(with_first, other_w, jnp.where(rest, high1, a1w))
    b0t = jnp.where(with_first, t0, jnp.where(rest, t1, b0t))
    b0w = jnp.where(with_first, sum0 - high0, jnp.where(rest, sum1 - high1, b0w))
    b1t = jnp.where(with_first, t0, jnp.where(rest, t1, t3))
    b1w = jnp.where(with_first | rest, b0w, w3)
    return (t0, a1t, b0t, b1t), (a0w, a1w, b0w, b1w)


def pack_kernel(
    ranks, ocean_blocks, col_hbm, col2_hbm, row2_hbm, weight_hbm, target_hbm,
    out_ref, col, col2, row2, weight_in, target_in, weight, target, sems,
):
    tiles = col.shape[0]
    lines, block = weight.shape
    halves = tiles // block
    stage_lines = lines // STAGES
    stage_tiles = tiles // STAGES
    col2_copy, row2_copy, col_copy = start_copies(((col2_hbm, col2), (row2_hbm, row2), (col_hbm, col)), sems)
    stages = []
    for i in range(STAGES):
        part = pl.ds(i * stage_lines, stage_lines)
        stages.append(
            start_copies(
                ((weight_hbm.at[part], weight_in.at[part]), (target_hbm.at[part], target_in.at[part])),
                sems.at[pl.ds(3 + 2 * i, 2)],
            )
        )

    col2_copy.wait()
    row2_copy.wait()
    slot = (col2[...] & 1) * ranks + (col2[...] >> 1)
    entry = lax.broadcasted_iota(I32, (8, block), 0)
    place = lax.broadcasted_iota(I32, (tiles, block), 0)
    onehot, values = [], []
    for h in range(halves):
        same = jnp.broadcast_to(slot[h : h + 1], (tiles, block)) == place
        onehot.append(jnp.where(same, 1.0, 0.0).astype(BF16))
        row = jnp.broadcast_to(row2[h : h + 1], (8, block))
        device = jnp.where(row >= 0, row // ocean_blocks + 1, 0)
        local = jnp.where(row >= 0, row % ocean_blocks, 0)
        values.append(jnp.where(entry == 0, local, device).astype(F32).astype(BF16))
    found = lax.dot_general(
        jnp.concatenate(values, 1), jnp.concatenate(onehot, 1), ROWS_WITH_ROWS, preferred_element_type=F32
    )
    device = jnp.maximum(found[1:2, :ranks], found[1:2, ranks:])
    low_lanes = lax.broadcasted_iota(I32, (1, block), 1) < ranks // 2
    first, second = found[0:1, :ranks], found[0:1, ranks:]
    locals_of = (
        jnp.where(low_lanes, first, pltpu.roll(second, ranks // 2, 1)),
        jnp.where(low_lanes, pltpu.roll(first, ranks // 2, 1), second),
    )
    for h in range(2):
        info = jnp.concatenate([device, locals_of[h]], 0).astype(BF16)

        def tell(s, carry, info=info):
            out_ref[s * CHUNK + 2 * TILE_PAIRS] = info
            return carry

        lax.fori_loop(h * ranks // 2, (h + 1) * ranks // 2, tell, 0, unroll=16)

    def widen(g, carry):
        at = pl.ds(pl.multiple_of(g * 16, 16), 16)
        weight[at] = weight_in[at].astype(F32)
        return carry

    def pair_up(g, carry):
        base = pl.multiple_of(g * 32, 32)
        at = [pl.ds(base + k, 8, ENTRIES) for k in range(ENTRIES)]
        targets, weights = regroup([target_in[a, :] for a in at], [weight[a, :] for a in at])
        for k in range(ENTRIES):
            target[at[k], :] = targets[k].astype(F32)
            weight[at[k], :] = weights[k]
        return carry

    def send(t, carry):
        home = col[t]
        base = (home >> 1) * CHUNK + (home & 1) * TILE_PAIRS
        line = pl.multiple_of(t * ENTRIES, ENTRIES)
        for h in range(2):
            at = pl.ds(line + 2 * h, 2)
            out_ref[base + h] = weight[at, :].astype(BF16)
            out_ref[base + 2 + h] = target[at, :].astype(BF16)
        return carry

    def each(part, size, body, unroll):
        count = stage_lines // size
        lax.fori_loop(part * count, (part + 1) * count, body, 0, unroll=unroll)

    for i in range(STAGES):
        stages[i][0].wait()
        each(i, 16, widen, 16)
        stages[i][1].wait()
        each(i, 32, pair_up, 8)
        if i == 0:
            col_copy.wait()
        each(i, ENTRIES, send, stage_tiles)


def flux_kernel(
    owner_hbm, bits_hbm, atm_hbm, sent_hbm, out, slot_hbm,
    owner, slot, count, bits, atm, ocean, sems,
):
    blocks, fields, block = atm.shape
    words = bits.shape[0]
    copies = start_copies(((owner_hbm, owner), (bits_hbm, bits), (atm_hbm, atm)), sems)

    def clear(c, carry):
        count[c] = 0
        return carry

    lax.fori_loop(0, count.shape[0], clear, 0, unroll=16)
    copies[0].wait()

    def home(b, carry):
        to = owner[b]
        rank = count[to]
        count[to] = rank + 1
        slot[b] = 2 * to + rank
        return carry

    lax.fori_loop(0, blocks, home, 0, unroll=8)
    slots_out = pltpu.make_async_copy(slot, slot_hbm, sems.at[3])
    slots_out.start()

    copies[1].wait()
    column = lax.broadcasted_iota(I32, (blocks, block), 1)
    word = column // 30
    packed = jnp.concatenate([bits[...], jnp.zeros((8 - words, blocks), I32)], 0).T
    picked = jnp.zeros((blocks, block), I32)
    for w in range(words):
        picked = jnp.where(word == w, jnp.broadcast_to(packed[:, w : w + 1], (blocks, block)), picked)
    ocean[...] = jnp.right_shift(picked, column - word * 30) & 1

    copies[2].wait()
    field = lax.broadcasted_iota(I32, (8, block), 0)

    def fluxes_of(b):
        state = atm[b, 0:16, :].astype(F32)
        head = state[0:8]
        wind_east = head[0:1]
        wind_north = head[1:2]
        speed = jnp.sqrt(wind_east * wind_east + wind_north * wind_north + 0.25)
        drive = jnp.where(field < 2, head, pltpu.roll(head, 6, 0) - head)
        is_ocean = jnp.broadcast_to(ocean[pl.ds(b, 1), :], (8, block)) == 1
        head = jnp.where(is_ocean & (field < 4), (0.5 * speed) * drive, head)
        return jnp.concatenate([jnp.concatenate([head, state[8:16]], 0).astype(BF16), atm[b, 16:fields, :]], 0)

    def pair(p, carry):
        out[p] = jnp.concatenate([fluxes_of(2 * p), fluxes_of(2 * p + 1)], 0).T
        return carry

    lax.fori_loop(0, blocks // 2, pair, 0, unroll=4)
    slots_out.wait()


def remap_kernel(
    ranks, slot_hbm, recv, flux, out_ref, owner_ref,
    slot, sum_even, sum_odd, rows_vmem, rows, sems,
):
    pairs, block, _ = flux.shape
    fields = out_ref.shape[1]
    copies = start_copies(((slot_hbm, slot),), sems)
    me = lax.axis_index("comp") * lax.axis_size("cpl") + lax.axis_index("cpl")
    lane = lax.broadcasted_iota(I32, (2, block), 1)
    other = ranks // 2
    mine = lax.rem(me, other)

    def hear(c, carry):
        local0, local1, device = carry
        info = recv[c * CHUNK + 2 * TILE_PAIRS].astype(F32)
        moved = pltpu.roll(info, lax.rem(c - mine + ranks, ranks), 1)
        local0 = jnp.maximum(local0, jnp.where(lane == c, moved, 0.0))
        local1 = jnp.maximum(local1, jnp.where(lane == (c ^ other), moved, 0.0))
        return local0, local1, jnp.maximum(device, info)

    zeros = jnp.zeros((2, block), F32)
    local0, local1, device = lax.fori_loop(0, ranks, hear, (zeros, zeros, zeros), unroll=ranks)
    padding = jnp.zeros((6, block), F32)
    rows_vmem[...] = jnp.concatenate([local0[1:2], local1[1:2], padding], 0).astype(I32)
    rows_in = pltpu.make_async_copy(rows_vmem, rows, sems.at[1])
    rows_in.start()
    owner_ref[...] = jnp.concatenate([device, padding], 0)
    sum_even[...] = jnp.zeros_like(sum_even)
    sum_odd[...] = jnp.zeros_like(sum_odd)
    column = lax.broadcasted_iota(I32, (block, block), 0).astype(F32).astype(BF16)
    nothing = jnp.zeros((), BF16)

    def spread(x):
        return jnp.broadcast_to(x, (block, block))

    def dense(b):
        home = slot[b]
        source = home >> 1
        rank = home & 1
        base = source * CHUNK + rank * TILE_PAIRS

        def two(h):
            weight = recv[base + h]
            target = recv[base + 2 + h]
            second = jnp.where(spread(target[1:2]) == column, spread(weight[1:2]), nothing)
            return jnp.where(spread(target[0:1]) == column, spread(weight[0:1]), second)

        return rows[rank, source ^ (rank * other)], jnp.concatenate([two(0), two(1)], 1)

    def pair(p, carry):
        row0, dense0 = dense(2 * p)
        row1, dense1 = dense(2 * p + 1)
        both = flux[p]
        terms = jnp.dot(
            jnp.concatenate([dense0, dense1], 0), jnp.concatenate([both, both], 0), preferred_element_type=F32
        )
        sum_even[row0] += terms[:block]
        sum_odd[row1] += terms[block:]
        return carry

    for copy in copies:
        copy.wait()
    rows_in.wait()
    lax.fori_loop(0, pairs, pair, 0, unroll=pairs)
    for q in range(out_ref.shape[0]):
        total = sum_even[q] + pltpu.roll(sum_odd[q], fields, 1)
        out_ref[q] = total.T[:fields]


def permute_kernel(owner_ref, x_ref, out_ref):
    ranks, pieces, block = x_ref.shape
    rows = ranks * pieces
    source = lax.broadcasted_iota(I32, (block, rows), 0)
    spread = lax.broadcasted_iota(I32, (block, rows), 1) // pieces == source
    owner = jnp.dot(
        owner_ref[...].astype(BF16), spread.astype(F32).astype(BF16), preferred_element_type=F32
    )[0:1]
    half = lax.broadcasted_iota(I32, (1, rows), 1) % pieces
    wanted = (owner.astype(I32) - 1) * pieces + half
    chosen = lax.broadcasted_iota(I32, (rows, rows), 0) == jnp.broadcast_to(wanted, (rows, rows))
    chosen = chosen.astype(F32).astype(BF16)
    value = x_ref[...].reshape(rows, block)
    high = value.astype(BF16)
    left = value - high.astype(F32)
    middle = left.astype(BF16)
    low = (left - middle.astype(F32)).astype(BF16)
    total = jnp.dot(chosen, high, preferred_element_type=F32)
    total += jnp.dot(chosen, middle, preferred_element_type=F32)
    total += jnp.dot(chosen, low, preferred_element_type=F32)
    out_ref[...] = total.reshape(ranks, pieces, block)


def hbm():
    return pl.BlockSpec(memory_space=pltpu.HBM)


def vmem():
    return pl.BlockSpec(memory_space=pltpu.VMEM)


def in_hbm(x):
    return pltpu.with_memory_space_constraint(x, pltpu.HBM)


def exchange(x):
    return lax.all_to_all(x, AXES, split_axis=0, concat_axis=0, tiled=True)


def on_device(atm_fields, land_bits, coupler_owner, tile_col, tile_row, tile_weight, tile_target):
    ranks = lax.axis_size("comp") * lax.axis_size("cpl")
    blocks, fields, block = atm_fields.shape
    words = land_bits.shape[1]
    tiles = tile_col.shape[0]
    lines = tiles * ENTRIES
    ocean_blocks = blocks // RATIO
    params = pltpu.CompilerParams(vmem_limit_bytes=VMEM_LIMIT)

    send = pl.pallas_call(
        lambda *refs: pack_kernel(ranks, ocean_blocks, *refs),
        out_shape=jax.ShapeDtypeStruct((ranks * CHUNK, 2, block), BF16),
        in_specs=[hbm()] * 5,
        out_specs=vmem(),
        scratch_shapes=[
            pltpu.SMEM((tiles,), I32),
            pltpu.VMEM((tiles // block, block), I32),
            pltpu.VMEM((tiles // block, block), I32),
            pltpu.VMEM((lines, block), BF16),
            pltpu.VMEM((lines, block), I32),
            pltpu.VMEM((lines, block), F32),
            pltpu.VMEM((lines, block), F32),
            pltpu.SemaphoreType.DMA((3 + 2 * STAGES,)),
        ],
        compiler_params=params,
        name="pack",
    )(
        in_hbm(tile_col),
        in_hbm(tile_col.reshape(tiles // block, block)),
        in_hbm(tile_row.reshape(tiles // block, block)),
        in_hbm(tile_weight.reshape(lines, block)),
        in_hbm(tile_target.reshape(lines, block)),
    )
    recv = exchange(send)

    fluxes, slot = pl.pallas_call(
        flux_kernel,
        out_shape=(pltpu.VMEM((blocks // 2, block, 2 * fields), BF16), pltpu.HBM((blocks,), I32)),
        in_specs=[hbm()] * 3 + [pl.BlockSpec(memory_space=pl.ANY)],
        out_specs=(vmem(), hbm()),
        scratch_shapes=[
            pltpu.SMEM((blocks,), I32),
            pltpu.SMEM((blocks,), I32),
            pltpu.SMEM((ranks,), I32),
            pltpu.VMEM((words, blocks), I32),
            pltpu.VMEM((blocks, fields, block), BF16),
            pltpu.VMEM((blocks, block), I32),
            pltpu.SemaphoreType.DMA((4,)),
        ],
        compiler_params=params,
        cost_estimate=pl.CostEstimate(flops=10_000_000, bytes_accessed=4_000_000, transcendentals=0),
        name="flux",
    )(in_hbm(coupler_owner), in_hbm(land_bits.T), in_hbm(atm_fields), send)

    sums, owner = pl.pallas_call(
        lambda *refs: remap_kernel(ranks, *refs),
        out_shape=(
            jax.ShapeDtypeStruct((ocean_blocks, fields, block), F32),
            jax.ShapeDtypeStruct((8, block), F32),
        ),
        in_specs=[hbm(), vmem(), vmem()],
        out_specs=(vmem(), vmem()),
        scratch_shapes=[
            pltpu.SMEM((blocks,), I32),
            pltpu.VMEM((ocean_blocks, block, 2 * fields), F32),
            pltpu.VMEM((ocean_blocks, block, 2 * fields), F32),
            pltpu.VMEM((8, block), I32),
            pltpu.SMEM((8, block), I32),
            pltpu.SemaphoreType.DMA((2,)),
        ],
        compiler_params=params,
        name="remap",
    )(in_hbm(slot), recv, fluxes)

    pieces = ocean_blocks * fields // ranks
    spread = exchange(sums.reshape(ranks, pieces, block))
    turned = pl.pallas_call(
        permute_kernel,
        out_shape=jax.ShapeDtypeStruct(spread.shape, F32),
        in_specs=[vmem(), vmem()],
        out_specs=vmem(),
        compiler_params=params,
        name="permute",
    )(owner, spread)
    return exchange(turned).reshape(ocean_blocks, fields, block)


def solution(mesh):
    in_specs = (
        P(AXES, None, None),
        P(AXES, None),
        P(AXES),
        P(AXES),
        P(AXES),
        P(AXES, None, None),
        P(AXES, None, None),
    )
    return jax.shard_map(
        on_device, mesh=mesh, in_specs=in_specs, out_specs=P(AXES, None, None), check_vma=False
    )
```

```python
import jax
import jax.numpy as jnp
from jax import lax
from jax.experimental import pallas as pl
from jax.experimental.pallas import tpu as pltpu
from jax.sharding import PartitionSpec as P

AXES = ("comp", "cpl")
ENTRIES = 4
RATIO = 32
CHUNK = 9
TILE_PAIRS = 4
STAGES = 4
VMEM_LIMIT = 24 * 1024 * 1024
BF16 = jnp.bfloat16
F32 = jnp.float32
I32 = jnp.int32
ROWS_WITH_ROWS = (((1,), (1,)), ((), ()))


def start_copies(pairs, sems):
    copies = [pltpu.make_async_copy(a, b, sems.at[i]) for i, (a, b) in enumerate(pairs)]
    for copy in copies:
        copy.start()
    return copies


def regroup(target, weight):
    t0, t1, t2, t3 = target
    w0, w1, w2, w3 = weight
    e01, e02, e03 = t0 == t1, t0 == t2, t0 == t3
    e12, e13, e23 = t1 == t2, t1 == t3, t2 == t3
    zero = jnp.zeros_like(w0)
    swap = e01 | e23
    a1t, a1w = jnp.where(swap, t2, t1), jnp.where(swap, w2, w1)
    b0t, b0w = jnp.where(swap, t1, t2), jnp.where(swap, w1, w2)
    with_first = (e01 & e02) | (e01 & e03) | (e02 & e03)
    rest = e12 & e13 & jnp.logical_not(with_first)
    sum0 = w0 + jnp.where(e01, w1, zero) + jnp.where(e02, w2, zero) + jnp.where(e03, w3, zero)
    sum1 = w1 + w2 + w3
    high0 = sum0.astype(BF16).astype(F32)
    high1 = sum1.astype(BF16).astype(F32)
    other_t = jnp.where(e01, jnp.where(e02, t3, t2), t1)
    other_w = jnp.where(e01, jnp.where(e02, w3, w2), w1)
    a0w = jnp.where(with_first, high0, w0)
    a1t = jnp.where(with_first, other_t, jnp.where(rest, t1, a1t))
    a1w = jnp.where(with_first, other_w, jnp.where(rest, high1, a1w))
    b0t = jnp.where(with_first, t0, jnp.where(rest, t1, b0t))
    b0w = jnp.where(with_first, sum0 - high0, jnp.where(rest, sum1 - high1, b0w))
    b1t = jnp.where(with_first, t0, jnp.where(rest, t1, t3))
    b1w = jnp.where(with_first | rest, b0w, w3)
    return (t0, a1t, b0t, b1t), (a0w, a1w, b0w, b1w)


def pack_kernel(
    ranks, ocean_blocks, col_hbm, col2_hbm, row2_hbm, weight_hbm, target_hbm,
    out_ref, col, col2, row2, weight_in, target_in, weight, target, sems,
):
    tiles = col.shape[0]
    lines, block = weight.shape
    halves = tiles // block
    stage_lines = lines // STAGES
    stage_tiles = tiles // STAGES
    col2_copy, row2_copy, col_copy = start_copies(((col2_hbm, col2), (row2_hbm, row2), (col_hbm, col)), sems)
    stages = []
    for i in range(STAGES):
        part = pl.ds(i * stage_lines, stage_lines)
        stages.append(
            start_copies(
                ((weight_hbm.at[part], weight_in.at[part]), (target_hbm.at[part], target_in.at[part])),
                sems.at[pl.ds(3 + 2 * i, 2)],
            )
        )

    col2_copy.wait()
    row2_copy.wait()
    slot = (col2[...] & 1) * ranks + (col2[...] >> 1)
    entry = lax.broadcasted_iota(I32, (8, block), 0)
    place = lax.broadcasted_iota(I32, (tiles, block), 0)
    onehot, values = [], []
    for h in range(halves):
        same = jnp.broadcast_to(slot[h : h + 1], (tiles, block)) == place
        onehot.append(jnp.where(same, 1.0, 0.0).astype(BF16))
        row = jnp.broadcast_to(row2[h : h + 1], (8, block))
        device = jnp.where(row >= 0, row // ocean_blocks + 1, 0)
        local = jnp.where(row >= 0, row % ocean_blocks, 0)
        values.append(jnp.where(entry == 0, local, device).astype(F32).astype(BF16))
    found = lax.dot_general(
        jnp.concatenate(values, 1), jnp.concatenate(onehot, 1), ROWS_WITH_ROWS, preferred_element_type=F32
    )
    device = jnp.maximum(found[1:2, :ranks], found[1:2, ranks:])
    low_lanes = lax.broadcasted_iota(I32, (1, block), 1) < ranks // 2
    first, second = found[0:1, :ranks], found[0:1, ranks:]
    locals_of = (
        jnp.where(low_lanes, first, pltpu.roll(second, ranks // 2, 1)),
        jnp.where(low_lanes, pltpu.roll(first, ranks // 2, 1), second),
    )
    for h in range(2):
        info = jnp.concatenate([device, locals_of[h]], 0).astype(BF16)

        def tell(s, carry, info=info):
            out_ref[s * CHUNK + 2 * TILE_PAIRS] = info
            return carry

        lax.fori_loop(h * ranks // 2, (h + 1) * ranks // 2, tell, 0, unroll=16)

    def widen(g, carry):
        at = pl.ds(pl.multiple_of(g * 16, 16), 16)
        weight[at] = weight_in[at].astype(F32)
        return carry

    def pair_up(g, carry):
        base = pl.multiple_of(g * 32, 32)
        at = [pl.ds(base + k, 8, ENTRIES) for k in range(ENTRIES)]
        targets, weights = regroup([target_in[a, :] for a in at], [weight[a, :] for a in at])
        for k in range(ENTRIES):
            target[at[k], :] = targets[k].astype(F32)
            weight[at[k], :] = weights[k]
        return carry

    def send(t, carry):
        home = col[t]
        base = (home >> 1) * CHUNK + (home & 1) * TILE_PAIRS
        line = pl.multiple_of(t * ENTRIES, ENTRIES)
        for h in range(2):
            at = pl.ds(line + 2 * h, 2)
            out_ref[base + h] = weight[at, :].astype(BF16)
            out_ref[base + 2 + h] = target[at, :].astype(BF16)
        return carry

    def each(part, size, body, unroll):
        count = stage_lines // size
        lax.fori_loop(part * count, (part + 1) * count, body, 0, unroll=unroll)

    for i in range(STAGES):
        stages[i][0].wait()
        each(i, 16, widen, 16)
        stages[i][1].wait()
        each(i, 32, pair_up, 8)
        if i == 0:
            col_copy.wait()
        each(i, ENTRIES, send, stage_tiles)


def flux_kernel(
    owner_hbm, bits_hbm, atm_hbm, sent_hbm, out, place_ref, onehot_ref,
    owner, bits, atm, ocean, sems,
):
    blocks, fields, block = atm.shape
    slots = onehot_ref.shape[0]
    ranks = slots // 2
    words = bits.shape[0]
    copies = start_copies(((owner_hbm, owner), (bits_hbm, bits), (atm_hbm, atm)), sems)

    copies[0].wait()
    to = jnp.broadcast_to(owner[...], (blocks, blocks))
    earlier = lax.broadcasted_iota(I32, (blocks, blocks), 0) < lax.broadcasted_iota(I32, (blocks, blocks), 1)
    rank = jnp.sum(jnp.where((to == to.T) & earlier, 1, 0), axis=0, keepdims=True)
    place_ref[...] = jnp.broadcast_to(owner[...] * CHUNK + rank * TILE_PAIRS, place_ref.shape)
    slot = jnp.broadcast_to(rank * ranks + owner[...], (slots, blocks))
    same = lax.broadcasted_iota(I32, (slots, blocks), 0) == slot
    onehot_ref[...] = jnp.where(same, 1.0, 0.0).astype(BF16)

    copies[1].wait()
    column = lax.broadcasted_iota(I32, (blocks, block), 1)
    word = column // 30
    packed = jnp.concatenate([bits[...], jnp.zeros((8 - words, blocks), I32)], 0).T
    picked = jnp.zeros((blocks, block), I32)
    for w in range(words):
        picked = jnp.where(word == w, jnp.broadcast_to(packed[:, w : w + 1], (blocks, block)), picked)
    ocean[...] = jnp.right_shift(picked, column - word * 30) & 1

    copies[2].wait()
    field = lax.broadcasted_iota(I32, (8, block), 0)

    def fluxes_of(b):
        state = atm[b, 0:16, :].astype(F32)
        head = state[0:8]
        wind_east = head[0:1]
        wind_north = head[1:2]
        speed = jnp.sqrt(wind_east * wind_east + wind_north * wind_north + 0.25)
        drive = jnp.where(field < 2, head, pltpu.roll(head, 6, 0) - head)
        is_ocean = jnp.broadcast_to(ocean[pl.ds(b, 1), :], (8, block)) == 1
        head = jnp.where(is_ocean & (field < 4), (0.5 * speed) * drive, head)
        return jnp.concatenate([jnp.concatenate([head, state[8:16]], 0).astype(BF16), atm[b, 16:fields, :]], 0)

    def pair(p, carry):
        out[p] = jnp.concatenate([fluxes_of(2 * p), fluxes_of(2 * p + 1)], 0).T
        return carry

    lax.fori_loop(0, blocks // 2, pair, 0, unroll=4)


def remap_kernel(
    ranks, place_ref, onehot_ref, recv, flux, out_ref, owner_ref, sum_even, sum_odd,
):
    pairs, block, _ = flux.shape
    fields = out_ref.shape[1]
    me = lax.axis_index("comp") * lax.axis_size("cpl") + lax.axis_index("cpl")
    lane = lax.broadcasted_iota(I32, (2, block), 1)
    other = ranks // 2
    mine = lax.rem(me, other)

    def hear(c, carry):
        local0, local1, device = carry
        info = recv[c * CHUNK + 2 * TILE_PAIRS].astype(F32)
        moved = pltpu.roll(info, lax.rem(c - mine + ranks, ranks), 1)
        local0 = jnp.maximum(local0, jnp.where(lane == c, moved, 0.0))
        local1 = jnp.maximum(local1, jnp.where(lane == (c ^ other), moved, 0.0))
        return local0, local1, jnp.maximum(device, info)

    zeros = jnp.zeros((2, block), F32)
    local0, local1, device = lax.fori_loop(0, ranks, hear, (zeros, zeros, zeros), unroll=ranks)
    owner_ref[...] = jnp.concatenate([device, jnp.zeros((6, block), F32)], 0)
    by_slot = jnp.concatenate([local0[1:2], pltpu.roll(local1, other, 1)[1:2]], 1)
    by_slot = jnp.broadcast_to(by_slot, (8, 2 * ranks)).astype(BF16)
    rows = jnp.dot(by_slot, onehot_ref[...], preferred_element_type=F32).astype(I32)
    shift = out_ref.shape[0].bit_length() - 1
    both_of = place_ref[...] * out_ref.shape[0] + rows
    sum_even[...] = jnp.zeros_like(sum_even)
    sum_odd[...] = jnp.zeros_like(sum_odd)
    column = lax.broadcasted_iota(I32, (block, block), 0).astype(F32).astype(BF16)
    nothing = jnp.zeros((), BF16)

    def spread(x):
        return jnp.broadcast_to(x, (block, block))

    def dense(base):
        def two(h):
            weight = recv[base + h]
            target = recv[base + 2 + h]
            second = jnp.where(spread(target[1:2]) == column, spread(weight[1:2]), nothing)
            return jnp.where(spread(target[0:1]) == column, spread(weight[0:1]), second)

        return jnp.concatenate([two(0), two(1)], 1)

    for p in range(pairs):
        at0 = both_of[0, 2 * p]
        at1 = both_of[0, 2 * p + 1]
        both = flux[p]
        terms = jnp.dot(
            jnp.concatenate([dense(at0 >> shift), dense(at1 >> shift)], 0),
            jnp.concatenate([both, both], 0),
            preferred_element_type=F32,
        )
        sum_even[at0 & (out_ref.shape[0] - 1)] += terms[:block]
        sum_odd[at1 & (out_ref.shape[0] - 1)] += terms[block:]
    for q in range(out_ref.shape[0]):
        total = sum_even[q] + pltpu.roll(sum_odd[q], fields, 1)
        out_ref[q] = total.T[:fields]


def permute_kernel(owner_ref, x_ref, out_ref):
    ranks, pieces, block = x_ref.shape
    owner = owner_ref[0:1].astype(I32) - 1
    chosen = lax.broadcasted_iota(I32, (ranks, ranks), 0) == jnp.broadcast_to(owner, (ranks, ranks))
    chosen = chosen.astype(F32).astype(BF16)
    value = jnp.concatenate([x_ref[:, k, :] for k in range(pieces)], 1)
    high = value.astype(BF16)
    left = value - high.astype(F32)
    middle = left.astype(BF16)
    low = (left - middle.astype(F32)).astype(BF16)
    total = jnp.dot(
        jnp.concatenate([chosen] * 3, 1), jnp.concatenate([high, middle, low], 0), preferred_element_type=F32
    )
    for k in range(pieces):
        out_ref[:, k, :] = total[:, k * block : (k + 1) * block]


def hbm():
    return pl.BlockSpec(memory_space=pltpu.HBM)


def vmem():
    return pl.BlockSpec(memory_space=pltpu.VMEM)


def in_hbm(x):
    return pltpu.with_memory_space_constraint(x, pltpu.HBM)


def exchange(x):
    return lax.all_to_all(x, AXES, split_axis=0, concat_axis=0, tiled=True)


def on_device(atm_fields, land_bits, coupler_owner, tile_col, tile_row, tile_weight, tile_target):
    ranks = lax.axis_size("comp") * lax.axis_size("cpl")
    blocks, fields, block = atm_fields.shape
    words = land_bits.shape[1]
    tiles = tile_col.shape[0]
    lines = tiles * ENTRIES
    ocean_blocks = blocks // RATIO
    params = pltpu.CompilerParams(vmem_limit_bytes=VMEM_LIMIT)

    send = pl.pallas_call(
        lambda *refs: pack_kernel(ranks, ocean_blocks, *refs),
        out_shape=jax.ShapeDtypeStruct((ranks * CHUNK, 2, block), BF16),
        in_specs=[hbm()] * 5,
        out_specs=vmem(),
        scratch_shapes=[
            pltpu.SMEM((tiles,), I32),
            pltpu.VMEM((tiles // block, block), I32),
            pltpu.VMEM((tiles // block, block), I32),
            pltpu.VMEM((lines, block), BF16),
            pltpu.VMEM((lines, block), I32),
            pltpu.VMEM((lines, block), F32),
            pltpu.VMEM((lines, block), F32),
            pltpu.SemaphoreType.DMA((3 + 2 * STAGES,)),
        ],
        compiler_params=params,
        name="pack",
    )(
        in_hbm(tile_col),
        in_hbm(tile_col.reshape(tiles // block, block)),
        in_hbm(tile_row.reshape(tiles // block, block)),
        in_hbm(tile_weight.reshape(lines, block)),
        in_hbm(tile_target.reshape(lines, block)),
    )
    recv = exchange(send)

    fluxes, place, onehot = pl.pallas_call(
        flux_kernel,
        out_shape=(
            pltpu.VMEM((blocks // 2, block, 2 * fields), BF16),
            pltpu.VMEM((8, blocks), I32),
            pltpu.VMEM((2 * ranks, blocks), BF16),
        ),
        in_specs=[hbm()] * 3 + [pl.BlockSpec(memory_space=pl.ANY)],
        out_specs=(vmem(), vmem(), vmem()),
        scratch_shapes=[
            pltpu.VMEM((1, blocks), I32),
            pltpu.VMEM((words, blocks), I32),
            pltpu.VMEM((blocks, fields, block), BF16),
            pltpu.VMEM((blocks, block), I32),
            pltpu.SemaphoreType.DMA((3,)),
        ],
        compiler_params=params,
        cost_estimate=pl.CostEstimate(flops=10_000_000, bytes_accessed=4_000_000, transcendentals=0),
        name="flux",
    )(in_hbm(coupler_owner.reshape(1, blocks)), in_hbm(land_bits.T), in_hbm(atm_fields), send)

    sums, owner = pl.pallas_call(
        lambda *refs: remap_kernel(ranks, *refs),
        out_shape=(
            jax.ShapeDtypeStruct((ocean_blocks, fields, block), F32),
            jax.ShapeDtypeStruct((8, block), F32),
        ),
        in_specs=[vmem()] * 4,
        out_specs=(vmem(), vmem()),
        scratch_shapes=[
            pltpu.VMEM((ocean_blocks, block, 2 * fields), F32),
            pltpu.VMEM((ocean_blocks, block, 2 * fields), F32),
        ],
        compiler_params=params,
        name="remap",
    )(place, onehot, recv, fluxes)

    pieces = ocean_blocks * fields // ranks
    spread = exchange(sums.reshape(ranks, pieces, block))
    turned = pl.pallas_call(
        permute_kernel,
        out_shape=jax.ShapeDtypeStruct(spread.shape, F32),
        in_specs=[vmem(), vmem()],
        out_specs=vmem(),
        compiler_params=params,
        name="permute",
    )(owner, spread)
    return exchange(turned).reshape(ocean_blocks, fields, block)


def solution(mesh):
    in_specs = (
        P(AXES, None, None),
        P(AXES, None),
        P(AXES),
        P(AXES),
        P(AXES),
        P(AXES, None, None),
        P(AXES, None, None),
    )
    return jax.shard_map(
        on_device, mesh=mesh, in_specs=in_specs, out_specs=P(AXES, None, None), check_vma=False
    )
```

```python
import jax
import jax.numpy as jnp
from jax import lax
from jax.experimental import pallas as pl
from jax.experimental.pallas import tpu as pltpu
from jax.sharding import PartitionSpec as P

AXES = ("comp", "cpl")
ENTRIES = 4
RATIO = 32
CHUNK = 9
TILE_PAIRS = 4
STAGES = 4
VMEM_LIMIT = 24 * 1024 * 1024
BF16 = jnp.bfloat16
F32 = jnp.float32
I32 = jnp.int32
ROWS_WITH_ROWS = (((1,), (1,)), ((), ()))


def start_copies(pairs, sems):
    copies = [pltpu.make_async_copy(a, b, sems.at[i]) for i, (a, b) in enumerate(pairs)]
    for copy in copies:
        copy.start()
    return copies


def regroup(target, weight):
    t0, t1, t2, t3 = target
    w0, w1, w2, w3 = weight
    e01, e02, e03 = t0 == t1, t0 == t2, t0 == t3
    e12, e13, e23 = t1 == t2, t1 == t3, t2 == t3
    zero = jnp.zeros_like(w0)
    swap = e01 | e23
    a1t, a1w = jnp.where(swap, t2, t1), jnp.where(swap, w2, w1)
    b0t, b0w = jnp.where(swap, t1, t2), jnp.where(swap, w1, w2)
    with_first = (e01 & e02) | (e01 & e03) | (e02 & e03)
    rest = e12 & e13 & jnp.logical_not(with_first)
    sum0 = w0 + jnp.where(e01, w1, zero) + jnp.where(e02, w2, zero) + jnp.where(e03, w3, zero)
    sum1 = w1 + w2 + w3
    high0 = sum0.astype(BF16).astype(F32)
    high1 = sum1.astype(BF16).astype(F32)
    other_t = jnp.where(e01, jnp.where(e02, t3, t2), t1)
    other_w = jnp.where(e01, jnp.where(e02, w3, w2), w1)
    a0w = jnp.where(with_first, high0, w0)
    a1t = jnp.where(with_first, other_t, jnp.where(rest, t1, a1t))
    a1w = jnp.where(with_first, other_w, jnp.where(rest, high1, a1w))
    b0t = jnp.where(with_first, t0, jnp.where(rest, t1, b0t))
    b0w = jnp.where(with_first, sum0 - high0, jnp.where(rest, sum1 - high1, b0w))
    b1t = jnp.where(with_first, t0, jnp.where(rest, t1, t3))
    b1w = jnp.where(with_first | rest, b0w, w3)
    return (t0, a1t, b0t, b1t), (a0w, a1w, b0w, b1w)


def pack_kernel(
    ranks, ocean_blocks, col_hbm, col2_hbm, row2_hbm, weight_hbm, target_hbm,
    out_ref, col, col2, row2, weight_in, target_in, weight, target, sems,
):
    tiles = col.shape[0]
    lines, block = weight.shape
    halves = tiles // block
    stage_lines = lines // STAGES
    stage_tiles = tiles // STAGES
    col2_copy, row2_copy, col_copy = start_copies(((col2_hbm, col2), (row2_hbm, row2), (col_hbm, col)), sems)
    stages = []
    for i in range(STAGES):
        part = pl.ds(i * stage_lines, stage_lines)
        stages.append(
            start_copies(
                ((weight_hbm.at[part], weight_in.at[part]), (target_hbm.at[part], target_in.at[part])),
                sems.at[pl.ds(3 + 2 * i, 2)],
            )
        )

    col2_copy.wait()
    row2_copy.wait()
    slot = (col2[...] & 1) * ranks + (col2[...] >> 1)
    entry = lax.broadcasted_iota(I32, (8, block), 0)
    place = lax.broadcasted_iota(I32, (tiles, block), 0).astype(F32).astype(BF16)
    slot = slot.astype(F32)
    one, nothing = jnp.ones((), BF16), jnp.zeros((), BF16)
    onehot, values = [], []
    for h in range(halves):
        same = jnp.broadcast_to(slot[h : h + 1].astype(BF16), (tiles, block)) == place
        onehot.append(jnp.where(same, one, nothing))
        row = jnp.broadcast_to(row2[h : h + 1], (8, block))
        device = jnp.where(row >= 0, row // ocean_blocks + 1, 0)
        local = jnp.where(row >= 0, row % ocean_blocks, 0)
        values.append(jnp.where(entry == 0, local, device).astype(F32).astype(BF16))
    found = lax.dot_general(
        jnp.concatenate(values, 1), jnp.concatenate(onehot, 1), ROWS_WITH_ROWS, preferred_element_type=F32
    )
    device = jnp.maximum(found[1:2, :ranks], found[1:2, ranks:])
    low_lanes = lax.broadcasted_iota(I32, (1, block), 1) < ranks // 2
    first, second = found[0:1, :ranks], found[0:1, ranks:]
    locals_of = (
        jnp.where(low_lanes, first, pltpu.roll(second, ranks // 2, 1)),
        jnp.where(low_lanes, pltpu.roll(first, ranks // 2, 1), second),
    )
    for h in range(2):
        info = jnp.concatenate([device, locals_of[h]], 0).astype(BF16)

        def tell(s, carry, info=info):
            out_ref[s * CHUNK + 2 * TILE_PAIRS] = info
            return carry

        lax.fori_loop(h * ranks // 2, (h + 1) * ranks // 2, tell, 0, unroll=16)

    def widen(g, carry):
        at = pl.ds(pl.multiple_of(g * 16, 16), 16)
        weight[at] = weight_in[at].astype(F32)
        return carry

    def pair_up(g, carry):
        base = pl.multiple_of(g * 32, 32)
        at = [pl.ds(base + k, 8, ENTRIES) for k in range(ENTRIES)]
        targets, weights = regroup([target_in[a, :] for a in at], [weight[a, :] for a in at])
        for k in range(ENTRIES):
            target[at[k], :] = targets[k].astype(F32)
            weight[at[k], :] = weights[k]
        return carry

    def send(t, carry):
        home = col[t]
        base = (home >> 1) * CHUNK + (home & 1) * TILE_PAIRS
        line = pl.multiple_of(t * ENTRIES, ENTRIES)
        for h in range(2):
            at = pl.ds(line + 2 * h, 2)
            out_ref[base + h] = weight[at, :].astype(BF16)
            out_ref[base + 2 + h] = target[at, :].astype(BF16)
        return carry

    def each(part, size, body, unroll):
        count = stage_lines // size
        lax.fori_loop(part * count, (part + 1) * count, body, 0, unroll=unroll)

    for i in range(STAGES):
        stages[i][0].wait()
        each(i, 16, widen, 16)
        stages[i][1].wait()
        each(i, 32, pair_up, 8)
        if i == 0:
            col_copy.wait()
        each(i, ENTRIES, send, stage_tiles)


def flux_kernel(
    owner_hbm, bits_hbm, atm_hbm, sent_hbm, out, place_ref, onehot_ref,
    owner, bits, atm, ocean, sems,
):
    blocks, fields, block = atm.shape
    slots = onehot_ref.shape[0]
    ranks = slots // 2
    words = bits.shape[0]
    copies = start_copies(((owner_hbm, owner), (bits_hbm, bits), (atm_hbm, atm)), sems)

    copies[0].wait()
    to = jnp.broadcast_to(owner[...], (blocks, blocks))
    earlier = lax.broadcasted_iota(I32, (blocks, blocks), 0) < lax.broadcasted_iota(I32, (blocks, blocks), 1)
    rank = jnp.sum(jnp.where((to == to.T) & earlier, 1, 0), axis=0, keepdims=True)
    place_ref[...] = jnp.broadcast_to(owner[...] * CHUNK + rank * TILE_PAIRS, place_ref.shape)
    slot = jnp.broadcast_to(rank * ranks + owner[...], (slots, blocks))
    same = lax.broadcasted_iota(I32, (slots, blocks), 0) == slot
    onehot_ref[...] = jnp.where(same, 1.0, 0.0).astype(BF16)

    copies[1].wait()
    column = lax.broadcasted_iota(I32, (blocks, block), 1)
    word = column // 30
    packed = jnp.concatenate([bits[...], jnp.zeros((8 - words, blocks), I32)], 0).T
    picked = jnp.zeros((blocks, block), I32)
    for w in range(words):
        picked = jnp.where(word == w, jnp.broadcast_to(packed[:, w : w + 1], (blocks, block)), picked)
    ocean[...] = jnp.right_shift(picked, column - word * 30) & 1

    copies[2].wait()
    field = lax.broadcasted_iota(I32, (8, block), 0)

    def fluxes_of(b):
        state = atm[b, 0:16, :].astype(F32)
        head = state[0:8]
        wind_east = head[0:1]
        wind_north = head[1:2]
        speed = jnp.sqrt(wind_east * wind_east + wind_north * wind_north + 0.25)
        drive = jnp.where(field < 2, head, pltpu.roll(head, 6, 0) - head)
        is_ocean = jnp.broadcast_to(ocean[pl.ds(b, 1), :], (8, block)) == 1
        head = jnp.where(is_ocean & (field < 4), (0.5 * speed) * drive, head)
        return jnp.concatenate([jnp.concatenate([head, state[8:16]], 0).astype(BF16), atm[b, 16:fields, :]], 0)

    def pair(p, carry):
        out[p] = jnp.concatenate([fluxes_of(2 * p), fluxes_of(2 * p + 1)], 0).T
        return carry

    lax.fori_loop(0, blocks // 2, pair, 0, unroll=4)


def remap_kernel(
    ranks, place_ref, onehot_ref, recv, flux, out_ref, owner_ref, sum_even, sum_odd,
):
    pairs, block, _ = flux.shape
    fields = out_ref.shape[1]
    me = lax.axis_index("comp") * lax.axis_size("cpl") + lax.axis_index("cpl")
    lane = lax.broadcasted_iota(I32, (2, block), 1)
    other = ranks // 2
    mine = lax.rem(me, other)

    def hear(c, carry):
        local0, local1, device = carry
        info = recv[c * CHUNK + 2 * TILE_PAIRS].astype(F32)
        moved = pltpu.roll(info, lax.rem(c - mine + ranks, ranks), 1)
        local0 = jnp.maximum(local0, jnp.where(lane == c, moved, 0.0))
        local1 = jnp.maximum(local1, jnp.where(lane == (c ^ other), moved, 0.0))
        return local0, local1, jnp.maximum(device, info)

    zeros = jnp.zeros((2, block), F32)
    local0, local1, device = lax.fori_loop(0, ranks, hear, (zeros, zeros, zeros), unroll=ranks)
    owner_ref[...] = jnp.concatenate([device, jnp.zeros((6, block), F32)], 0)
    by_slot = jnp.concatenate([local0[1:2], pltpu.roll(local1, other, 1)[1:2]], 1)
    by_slot = jnp.broadcast_to(by_slot, (8, 2 * ranks)).astype(BF16)
    rows = jnp.dot(by_slot, onehot_ref[...], preferred_element_type=F32).astype(I32)
    shift = out_ref.shape[0].bit_length() - 1
    both_of = place_ref[...] * out_ref.shape[0] + rows
    sum_even[...] = jnp.zeros_like(sum_even)
    sum_odd[...] = jnp.zeros_like(sum_odd)
    column = lax.broadcasted_iota(I32, (block, block), 0).astype(F32).astype(BF16)
    nothing = jnp.zeros((), BF16)

    def spread(x):
        return jnp.broadcast_to(x, (block, block))

    def dense(base):
        def two(h):
            weight = recv[base + h]
            target = recv[base + 2 + h]
            second = jnp.where(spread(target[1:2]) == column, spread(weight[1:2]), nothing)
            return jnp.where(spread(target[0:1]) == column, spread(weight[0:1]), second)

        return jnp.concatenate([two(0), two(1)], 1)

    for p in range(pairs):
        at0 = both_of[0, 2 * p]
        at1 = both_of[0, 2 * p + 1]
        both = flux[p]
        terms = jnp.dot(
            jnp.concatenate([dense(at0 >> shift), dense(at1 >> shift)], 0),
            jnp.concatenate([both, both], 0),
            preferred_element_type=F32,
        )
        sum_even[at0 & (out_ref.shape[0] - 1)] += terms[:block]
        sum_odd[at1 & (out_ref.shape[0] - 1)] += terms[block:]
    low_lanes = lax.broadcasted_iota(I32, (block, 2 * fields), 1) < fields
    for q in range(0, out_ref.shape[0], 2):
        total = jnp.where(low_lanes, sum_even[q], sum_odd[q + 1])
        total += pltpu.roll(jnp.where(low_lanes, sum_even[q + 1], sum_odd[q]), fields, 1)
        both = total.T
        out_ref[q] = both[:fields]
        out_ref[q + 1] = both[fields:]


def permute_kernel(owner_ref, x_ref, out_ref):
    ranks, pieces, block = x_ref.shape
    owner = owner_ref[0:1].astype(I32) - 1
    chosen = lax.broadcasted_iota(I32, (ranks, ranks), 0) == jnp.broadcast_to(owner, (ranks, ranks))
    chosen = chosen.astype(F32).astype(BF16)
    value = jnp.concatenate([x_ref[:, k, :] for k in range(pieces)], 1)
    high = value.astype(BF16)
    left = value - high.astype(F32)
    middle = left.astype(BF16)
    low = (left - middle.astype(F32)).astype(BF16)
    total = jnp.dot(
        jnp.concatenate([chosen] * 3, 1), jnp.concatenate([high, middle, low], 0), preferred_element_type=F32
    )
    for k in range(pieces):
        out_ref[:, k, :] = total[:, k * block : (k + 1) * block]


def hbm():
    return pl.BlockSpec(memory_space=pltpu.HBM)


def vmem():
    return pl.BlockSpec(memory_space=pltpu.VMEM)


def in_hbm(x):
    return pltpu.with_memory_space_constraint(x, pltpu.HBM)


def exchange(x):
    return lax.all_to_all(x, AXES, split_axis=0, concat_axis=0, tiled=True)


def on_device(atm_fields, land_bits, coupler_owner, tile_col, tile_row, tile_weight, tile_target):
    ranks = lax.axis_size("comp") * lax.axis_size("cpl")
    blocks, fields, block = atm_fields.shape
    words = land_bits.shape[1]
    tiles = tile_col.shape[0]
    lines = tiles * ENTRIES
    ocean_blocks = blocks // RATIO
    params = pltpu.CompilerParams(vmem_limit_bytes=VMEM_LIMIT)

    send = pl.pallas_call(
        lambda *refs: pack_kernel(ranks, ocean_blocks, *refs),
        out_shape=jax.ShapeDtypeStruct((ranks * CHUNK, 2, block), BF16),
        in_specs=[hbm()] * 5,
        out_specs=vmem(),
        scratch_shapes=[
            pltpu.SMEM((tiles,), I32),
            pltpu.VMEM((tiles // block, block), I32),
            pltpu.VMEM((tiles // block, block), I32),
            pltpu.VMEM((lines, block), BF16),
            pltpu.VMEM((lines, block), I32),
            pltpu.VMEM((lines, block), F32),
            pltpu.VMEM((lines, block), F32),
            pltpu.SemaphoreType.DMA((3 + 2 * STAGES,)),
        ],
        compiler_params=params,
        name="pack",
    )(
        in_hbm(tile_col),
        in_hbm(tile_col.reshape(tiles // block, block)),
        in_hbm(tile_row.reshape(tiles // block, block)),
        in_hbm(tile_weight.reshape(lines, block)),
        in_hbm(tile_target.reshape(lines, block)),
    )
    recv = exchange(send)

    fluxes, place, onehot = pl.pallas_call(
        flux_kernel,
        out_shape=(
            pltpu.VMEM((blocks // 2, block, 2 * fields), BF16),
            pltpu.VMEM((8, blocks), I32),
            pltpu.VMEM((2 * ranks, blocks), BF16),
        ),
        in_specs=[hbm()] * 3 + [pl.BlockSpec(memory_space=pl.ANY)],
        out_specs=(vmem(), vmem(), vmem()),
        scratch_shapes=[
            pltpu.VMEM((1, blocks), I32),
            pltpu.VMEM((words, blocks), I32),
            pltpu.VMEM((blocks, fields, block), BF16),
            pltpu.VMEM((blocks, block), I32),
            pltpu.SemaphoreType.DMA((3,)),
        ],
        compiler_params=params,
        cost_estimate=pl.CostEstimate(flops=10_000_000, bytes_accessed=4_000_000, transcendentals=0),
        name="flux",
    )(in_hbm(coupler_owner.reshape(1, blocks)), in_hbm(land_bits.T), in_hbm(atm_fields), send)

    sums, owner = pl.pallas_call(
        lambda *refs: remap_kernel(ranks, *refs),
        out_shape=(
            jax.ShapeDtypeStruct((ocean_blocks, fields, block), F32),
            jax.ShapeDtypeStruct((8, block), F32),
        ),
        in_specs=[vmem()] * 4,
        out_specs=(vmem(), vmem()),
        scratch_shapes=[
            pltpu.VMEM((ocean_blocks, block, 2 * fields), F32),
            pltpu.VMEM((ocean_blocks, block, 2 * fields), F32),
        ],
        compiler_params=params,
        name="remap",
    )(place, onehot, recv, fluxes)

    pieces = ocean_blocks * fields // ranks
    spread = exchange(sums.reshape(ranks, pieces, block))
    turned = pl.pallas_call(
        permute_kernel,
        out_shape=jax.ShapeDtypeStruct(spread.shape, F32),
        in_specs=[vmem(), vmem()],
        out_specs=vmem(),
        compiler_params=params,
        name="permute",
    )(owner, spread)
    return exchange(turned).reshape(ocean_blocks, fields, block)


def solution(mesh):
    in_specs = (
        P(AXES, None, None),
        P(AXES, None),
        P(AXES),
        P(AXES),
        P(AXES),
        P(AXES, None, None),
        P(AXES, None, None),
    )
    return jax.shard_map(
        on_device, mesh=mesh, in_specs=in_specs, out_specs=P(AXES, None, None), check_vma=False
    )
```

```python
import jax
import jax.numpy as jnp
from jax import lax
from jax.experimental import pallas as pl
from jax.experimental.pallas import tpu as pltpu
from jax.sharding import PartitionSpec as P

AXES = ("comp", "cpl")
ENTRIES = 4
RATIO = 32
CHUNK = 9
TILE_PAIRS = 4
STAGES = 4
VMEM_LIMIT = 24 * 1024 * 1024
BF16 = jnp.bfloat16
F32 = jnp.float32
I32 = jnp.int32
ROWS_WITH_ROWS = (((1,), (1,)), ((), ()))


def start_copies(pairs, sems):
    copies = [pltpu.make_async_copy(a, b, sems.at[i]) for i, (a, b) in enumerate(pairs)]
    for copy in copies:
        copy.start()
    return copies


def regroup(target, weight):
    t0, t1, t2, t3 = target
    w0, w1, w2, w3 = weight
    e01, e02, e03 = t0 == t1, t0 == t2, t0 == t3
    e12, e13, e23 = t1 == t2, t1 == t3, t2 == t3
    zero = jnp.zeros_like(w0)
    swap = e01 | e23
    a1t, a1w = jnp.where(swap, t2, t1), jnp.where(swap, w2, w1)
    b0t, b0w = jnp.where(swap, t1, t2), jnp.where(swap, w1, w2)
    with_first = (e01 & e02) | (e01 & e03) | (e02 & e03)
    rest = e12 & e13 & jnp.logical_not(with_first)
    sum0 = w0 + jnp.where(e01, w1, zero) + jnp.where(e02, w2, zero) + jnp.where(e03, w3, zero)
    sum1 = w1 + w2 + w3
    high0 = sum0.astype(BF16).astype(F32)
    high1 = sum1.astype(BF16).astype(F32)
    other_t = jnp.where(e01, jnp.where(e02, t3, t2), t1)
    other_w = jnp.where(e01, jnp.where(e02, w3, w2), w1)
    a0w = jnp.where(with_first, high0, w0)
    a1t = jnp.where(with_first, other_t, jnp.where(rest, t1, a1t))
    a1w = jnp.where(with_first, other_w, jnp.where(rest, high1, a1w))
    b0t = jnp.where(with_first, t0, jnp.where(rest, t1, b0t))
    b0w = jnp.where(with_first, sum0 - high0, jnp.where(rest, sum1 - high1, b0w))
    b1t = jnp.where(with_first, t0, jnp.where(rest, t1, t3))
    b1w = jnp.where(with_first | rest, b0w, w3)
    return (t0, a1t, b0t, b1t), (a0w, a1w, b0w, b1w)


def pack_kernel(
    ranks, ocean_blocks, col_hbm, col2_hbm, row2_hbm, weight_hbm, target_hbm,
    out_ref, col, col2, row2, weight_in, target_in, weight, target, sems,
):
    tiles = col.shape[0]
    lines, block = weight.shape
    halves = tiles // block
    stage_lines = lines // STAGES
    stage_tiles = tiles // STAGES
    col2_copy, row2_copy, col_copy = start_copies(((col2_hbm, col2), (row2_hbm, row2), (col_hbm, col)), sems)
    stages = []
    for i in range(STAGES):
        part = pl.ds(i * stage_lines, stage_lines)
        stages.append(
            start_copies(
                ((weight_hbm.at[part], weight_in.at[part]), (target_hbm.at[part], target_in.at[part])),
                sems.at[pl.ds(3 + 2 * i, 2)],
            )
        )

    col2_copy.wait()
    row2_copy.wait()
    slot = (col2[...] & 1) * ranks + (col2[...] >> 1)
    entry = lax.broadcasted_iota(I32, (8, block), 0)
    place = lax.broadcasted_iota(I32, (tiles, block), 0).astype(F32).astype(BF16)
    slot = slot.astype(F32)
    one, nothing = jnp.ones((), BF16), jnp.zeros((), BF16)
    onehot, values = [], []
    for h in range(halves):
        same = jnp.broadcast_to(slot[h : h + 1].astype(BF16), (tiles, block)) == place
        onehot.append(jnp.where(same, one, nothing))
        row = jnp.broadcast_to(row2[h : h + 1], (8, block))
        device = jnp.where(row >= 0, row // ocean_blocks + 1, 0)
        local = jnp.where(row >= 0, row % ocean_blocks, 0)
        values.append(jnp.where(entry == 0, local, device).astype(F32).astype(BF16))
    found = lax.dot_general(
        jnp.concatenate(values, 1), jnp.concatenate(onehot, 1), ROWS_WITH_ROWS, preferred_element_type=F32
    )
    device = jnp.maximum(found[1:2, :ranks], found[1:2, ranks:])
    low_lanes = lax.broadcasted_iota(I32, (1, block), 1) < ranks // 2
    first, second = found[0:1, :ranks], found[0:1, ranks:]
    locals_of = (
        jnp.where(low_lanes, first, pltpu.roll(second, ranks // 2, 1)),
        jnp.where(low_lanes, pltpu.roll(first, ranks // 2, 1), second),
    )
    for h in range(2):
        info = jnp.concatenate([device, locals_of[h]], 0).astype(BF16)

        def tell(s, carry, info=info):
            out_ref[s * CHUNK + 2 * TILE_PAIRS] = info
            return carry

        lax.fori_loop(h * ranks // 2, (h + 1) * ranks // 2, tell, 0, unroll=16)

    def widen(g, carry):
        at = pl.ds(pl.multiple_of(g * 16, 16), 16)
        weight[at] = weight_in[at].astype(F32)
        return carry

    def pair_up(g, carry):
        base = pl.multiple_of(g * 32, 32)
        at = [pl.ds(base + k, 8, ENTRIES) for k in range(ENTRIES)]
        targets, weights = regroup([target_in[a, :] for a in at], [weight[a, :] for a in at])
        for k in range(ENTRIES):
            target[at[k], :] = targets[k].astype(F32)
            weight[at[k], :] = weights[k]
        return carry

    def send(t, carry):
        home = col[t]
        base = (home >> 1) * CHUNK + (home & 1) * TILE_PAIRS
        line = pl.multiple_of(t * ENTRIES, ENTRIES)
        for h in range(2):
            at = pl.ds(line + 2 * h, 2)
            out_ref[base + h] = weight[at, :].astype(BF16)
            out_ref[base + 2 + h] = target[at, :].astype(BF16)
        return carry

    def each(part, size, body, unroll):
        count = stage_lines // size
        lax.fori_loop(part * count, (part + 1) * count, body, 0, unroll=unroll)

    for i in range(STAGES):
        stages[i][0].wait()
        each(i, 16, widen, 16)
        stages[i][1].wait()
        each(i, 32, pair_up, 8)
        if i == 0:
            col_copy.wait()
        each(i, ENTRIES, send, stage_tiles)


def flux_kernel(
    owner_hbm, bits_hbm, atm_hbm, sent_hbm, out, slot_hbm,
    owner, slot, count, bits, atm, ocean, sems,
):
    blocks, fields, block = atm.shape
    words = bits.shape[0]
    copies = start_copies(((owner_hbm, owner), (bits_hbm, bits), (atm_hbm, atm)), sems)

    def clear(c, carry):
        count[c] = 0
        return carry

    lax.fori_loop(0, count.shape[0], clear, 0, unroll=16)
    copies[0].wait()

    def home(b, carry):
        to = owner[b]
        rank = count[to]
        count[to] = rank + 1
        slot[b] = 2 * to + rank
        return carry

    lax.fori_loop(0, blocks, home, 0, unroll=8)
    slots_out = pltpu.make_async_copy(slot, slot_hbm, sems.at[3])
    slots_out.start()

    copies[1].wait()
    column = lax.broadcasted_iota(I32, (blocks, block), 1)
    word = column // 30
    packed = jnp.concatenate([bits[...], jnp.zeros((8 - words, blocks), I32)], 0).T
    picked = jnp.zeros((blocks, block), I32)
    for w in range(words):
        picked = jnp.where(word == w, jnp.broadcast_to(packed[:, w : w + 1], (blocks, block)), picked)
    ocean[...] = jnp.right_shift(picked, column - word * 30) & 1

    copies[2].wait()
    field = lax.broadcasted_iota(I32, (8, block), 0)

    def fluxes_of(b):
        state = atm[b, 0:16, :].astype(F32)
        head = state[0:8]
        wind_east = head[0:1]
        wind_north = head[1:2]
        speed = jnp.sqrt(wind_east * wind_east + wind_north * wind_north + 0.25)
        drive = jnp.where(field < 2, head, pltpu.roll(head, 6, 0) - head)
        is_ocean = jnp.broadcast_to(ocean[pl.ds(b, 1), :], (8, block)) == 1
        head = jnp.where(is_ocean & (field < 4), (0.5 * speed) * drive, head)
        return jnp.concatenate([jnp.concatenate([head, state[8:16]], 0).astype(BF16), atm[b, 16:fields, :]], 0)

    def pair(p, carry):
        out[p] = jnp.concatenate([fluxes_of(2 * p), fluxes_of(2 * p + 1)], 0).T
        return carry

    lax.fori_loop(0, blocks // 2, pair, 0, unroll=4)
    slots_out.wait()


def remap_kernel(
    ranks, slot_hbm, recv, flux, out_ref, owner_ref,
    slot, sum_even, sum_odd, rows_vmem, rows, sems,
):
    pairs, block, _ = flux.shape
    fields = out_ref.shape[1]
    copies = start_copies(((slot_hbm, slot),), sems)
    me = lax.axis_index("comp") * lax.axis_size("cpl") + lax.axis_index("cpl")
    lane = lax.broadcasted_iota(I32, (2, block), 1)
    other = ranks // 2
    mine = lax.rem(me, other)

    def hear(c, carry):
        local0, local1, device = carry
        info = recv[c * CHUNK + 2 * TILE_PAIRS].astype(F32)
        moved = pltpu.roll(info, lax.rem(c - mine + ranks, ranks), 1)
        local0 = jnp.maximum(local0, jnp.where(lane == c, moved, 0.0))
        local1 = jnp.maximum(local1, jnp.where(lane == (c ^ other), moved, 0.0))
        return local0, local1, jnp.maximum(device, info)

    zeros = jnp.zeros((2, block), F32)
    local0, local1, device = lax.fori_loop(0, ranks, hear, (zeros, zeros, zeros), unroll=ranks)
    padding = jnp.zeros((6, block), F32)
    rows_vmem[...] = jnp.concatenate([local0[1:2], local1[1:2], padding], 0).astype(I32)
    rows_in = pltpu.make_async_copy(rows_vmem, rows, sems.at[1])
    rows_in.start()
    owner_ref[...] = jnp.concatenate([device, padding], 0)
    sum_even[...] = jnp.zeros_like(sum_even)
    sum_odd[...] = jnp.zeros_like(sum_odd)
    column = lax.broadcasted_iota(I32, (block, block), 0).astype(F32).astype(BF16)
    nothing = jnp.zeros((), BF16)

    def spread(x):
        return jnp.broadcast_to(x, (block, block))

    def dense(b):
        home = slot[b]
        source = home >> 1
        rank = home & 1
        base = source * CHUNK + rank * TILE_PAIRS

        def two(h):
            weight = recv[base + h]
            target = recv[base + 2 + h]
            second = jnp.where(spread(target[1:2]) == column, spread(weight[1:2]), nothing)
            return jnp.where(spread(target[0:1]) == column, spread(weight[0:1]), second)

        return rows[rank, source ^ (rank * other)], jnp.concatenate([two(0), two(1)], 1)

    def pair(p, carry):
        row0, dense0 = dense(2 * p)
        row1, dense1 = dense(2 * p + 1)
        both = flux[p]
        terms = jnp.dot(
            jnp.concatenate([dense0, dense1], 0), jnp.concatenate([both, both], 0), preferred_element_type=F32
        )
        sum_even[row0] += terms[:block]
        sum_odd[row1] += terms[block:]
        return carry

    for copy in copies:
        copy.wait()
    rows_in.wait()
    lax.fori_loop(0, pairs, pair, 0, unroll=pairs)
    low_lanes = lax.broadcasted_iota(I32, (block, 2 * fields), 1) < fields
    for q in range(0, out_ref.shape[0], 2):
        total = jnp.where(low_lanes, sum_even[q], sum_odd[q + 1])
        total += pltpu.roll(jnp.where(low_lanes, sum_even[q + 1], sum_odd[q]), fields, 1)
        both = total.T
        out_ref[q] = both[:fields]
        out_ref[q + 1] = both[fields:]


def permute_kernel(owner_ref, x_ref, out_ref):
    ranks, pieces, block = x_ref.shape
    owner = owner_ref[0:1].astype(I32) - 1
    chosen = lax.broadcasted_iota(I32, (ranks, ranks), 0) == jnp.broadcast_to(owner, (ranks, ranks))
    chosen = chosen.astype(F32).astype(BF16)
    value = jnp.concatenate([x_ref[:, k, :] for k in range(pieces)], 1)
    high = value.astype(BF16)
    left = value - high.astype(F32)
    middle = left.astype(BF16)
    low = (left - middle.astype(F32)).astype(BF16)
    total = jnp.dot(
        jnp.concatenate([chosen] * 3, 1), jnp.concatenate([high, middle, low], 0), preferred_element_type=F32
    )
    for k in range(pieces):
        out_ref[:, k, :] = total[:, k * block : (k + 1) * block]


def hbm():
    return pl.BlockSpec(memory_space=pltpu.HBM)


def vmem():
    return pl.BlockSpec(memory_space=pltpu.VMEM)


def in_hbm(x):
    return pltpu.with_memory_space_constraint(x, pltpu.HBM)


def exchange(x):
    return lax.all_to_all(x, AXES, split_axis=0, concat_axis=0, tiled=True)


def on_device(atm_fields, land_bits, coupler_owner, tile_col, tile_row, tile_weight, tile_target):
    ranks = lax.axis_size("comp") * lax.axis_size("cpl")
    blocks, fields, block = atm_fields.shape
    words = land_bits.shape[1]
    tiles = tile_col.shape[0]
    lines = tiles * ENTRIES
    ocean_blocks = blocks // RATIO
    params = pltpu.CompilerParams(vmem_limit_bytes=VMEM_LIMIT)

    send = pl.pallas_call(
        lambda *refs: pack_kernel(ranks, ocean_blocks, *refs),
        out_shape=jax.ShapeDtypeStruct((ranks * CHUNK, 2, block), BF16),
        in_specs=[hbm()] * 5,
        out_specs=vmem(),
        scratch_shapes=[
            pltpu.SMEM((tiles,), I32),
            pltpu.VMEM((tiles // block, block), I32),
            pltpu.VMEM((tiles // block, block), I32),
            pltpu.VMEM((lines, block), BF16),
            pltpu.VMEM((lines, block), I32),
            pltpu.VMEM((lines, block), F32),
            pltpu.VMEM((lines, block), F32),
            pltpu.SemaphoreType.DMA((3 + 2 * STAGES,)),
        ],
        compiler_params=params,
        name="pack",
    )(
        in_hbm(tile_col),
        in_hbm(tile_col.reshape(tiles // block, block)),
        in_hbm(tile_row.reshape(tiles // block, block)),
        in_hbm(tile_weight.reshape(lines, block)),
        in_hbm(tile_target.reshape(lines, block)),
    )
    recv = exchange(send)

    fluxes, slot = pl.pallas_call(
        flux_kernel,
        out_shape=(pltpu.VMEM((blocks // 2, block, 2 * fields), BF16), pltpu.HBM((blocks,), I32)),
        in_specs=[hbm()] * 3 + [pl.BlockSpec(memory_space=pl.ANY)],
        out_specs=(vmem(), hbm()),
        scratch_shapes=[
            pltpu.SMEM((blocks,), I32),
            pltpu.SMEM((blocks,), I32),
            pltpu.SMEM((ranks,), I32),
            pltpu.VMEM((words, blocks), I32),
            pltpu.VMEM((blocks, fields, block), BF16),
            pltpu.VMEM((blocks, block), I32),
            pltpu.SemaphoreType.DMA((4,)),
        ],
        compiler_params=params,
        cost_estimate=pl.CostEstimate(flops=10_000_000, bytes_accessed=4_000_000, transcendentals=0),
        name="flux",
    )(in_hbm(coupler_owner), in_hbm(land_bits.T), in_hbm(atm_fields), send)

    sums, owner = pl.pallas_call(
        lambda *refs: remap_kernel(ranks, *refs),
        out_shape=(
            jax.ShapeDtypeStruct((ocean_blocks, fields, block), F32),
            jax.ShapeDtypeStruct((8, block), F32),
        ),
        in_specs=[hbm(), vmem(), vmem()],
        out_specs=(vmem(), vmem()),
        scratch_shapes=[
            pltpu.SMEM((blocks,), I32),
            pltpu.VMEM((ocean_blocks, block, 2 * fields), F32),
            pltpu.VMEM((ocean_blocks, block, 2 * fields), F32),
            pltpu.VMEM((8, block), I32),
            pltpu.SMEM((8, block), I32),
            pltpu.SemaphoreType.DMA((2,)),
        ],
        compiler_params=params,
        name="remap",
    )(in_hbm(slot), recv, fluxes)

    pieces = ocean_blocks * fields // ranks
    spread = exchange(sums.reshape(ranks, pieces, block))
    turned = pl.pallas_call(
        permute_kernel,
        out_shape=jax.ShapeDtypeStruct(spread.shape, F32),
        in_specs=[vmem(), vmem()],
        out_specs=vmem(),
        compiler_params=params,
        name="permute",
    )(owner, spread)
    return exchange(turned).reshape(ocean_blocks, fields, block)


def solution(mesh):
    in_specs = (
        P(AXES, None, None),
        P(AXES, None),
        P(AXES),
        P(AXES),
        P(AXES),
        P(AXES, None, None),
        P(AXES, None, None),
    )
    return jax.shard_map(
        on_device, mesh=mesh, in_specs=in_specs, out_specs=P(AXES, None, None), check_vma=False
    )
```

```python
import jax
import jax.numpy as jnp
from jax import lax
from jax.experimental import pallas as pl
from jax.experimental.pallas import tpu as pltpu
from jax.sharding import PartitionSpec as P

AXES = ("comp", "cpl")
ENTRIES = 4
RATIO = 32
CHUNK = 9
TILE_PAIRS = 4
STAGES = 4
VMEM_LIMIT = 24 * 1024 * 1024
BF16 = jnp.bfloat16
F32 = jnp.float32
I32 = jnp.int32
ROWS_WITH_ROWS = (((1,), (1,)), ((), ()))


def start_copies(pairs, sems):
    copies = [pltpu.make_async_copy(a, b, sems.at[i]) for i, (a, b) in enumerate(pairs)]
    for copy in copies:
        copy.start()
    return copies


def regroup(target, weight):
    t0, t1, t2, t3 = target
    w0, w1, w2, w3 = weight
    e01, e02, e03 = t0 == t1, t0 == t2, t0 == t3
    e12, e13, e23 = t1 == t2, t1 == t3, t2 == t3
    zero = jnp.zeros_like(w0)
    swap = e01 | e23
    a1t, a1w = jnp.where(swap, t2, t1), jnp.where(swap, w2, w1)
    b0t, b0w = jnp.where(swap, t1, t2), jnp.where(swap, w1, w2)
    with_first = (e01 & e02) | (e01 & e03) | (e02 & e03)
    rest = e12 & e13 & jnp.logical_not(with_first)
    sum0 = w0 + jnp.where(e01, w1, zero) + jnp.where(e02, w2, zero) + jnp.where(e03, w3, zero)
    sum1 = w1 + w2 + w3
    high0 = sum0.astype(BF16).astype(F32)
    high1 = sum1.astype(BF16).astype(F32)
    other_t = jnp.where(e01, jnp.where(e02, t3, t2), t1)
    other_w = jnp.where(e01, jnp.where(e02, w3, w2), w1)
    a0w = jnp.where(with_first, high0, w0)
    a1t = jnp.where(with_first, other_t, jnp.where(rest, t1, a1t))
    a1w = jnp.where(with_first, other_w, jnp.where(rest, high1, a1w))
    b0t = jnp.where(with_first, t0, jnp.where(rest, t1, b0t))
    b0w = jnp.where(with_first, sum0 - high0, jnp.where(rest, sum1 - high1, b0w))
    b1t = jnp.where(with_first, t0, jnp.where(rest, t1, t3))
    b1w = jnp.where(with_first | rest, b0w, w3)
    return (t0, a1t, b0t, b1t), (a0w, a1w, b0w, b1w)


def pack_kernel(
    ranks, ocean_blocks, col_hbm, col2_hbm, row2_hbm, weight_hbm, target_hbm,
    out_ref, col, col2, row2, weight_in, target_in, weight, target, sems,
):
    tiles = col.shape[0]
    lines, block = weight.shape
    halves = tiles // block
    stage_lines = lines // STAGES
    stage_tiles = tiles // STAGES
    col2_copy, row2_copy, col_copy = start_copies(((col2_hbm, col2), (row2_hbm, row2), (col_hbm, col)), sems)
    stages = []
    for i in range(STAGES):
        part = pl.ds(i * stage_lines, stage_lines)
        stages.append(
            start_copies(
                ((weight_hbm.at[part], weight_in.at[part]), (target_hbm.at[part], target_in.at[part])),
                sems.at[pl.ds(3 + 2 * i, 2)],
            )
        )

    col2_copy.wait()
    row2_copy.wait()
    slot = (col2[...] & 1) * ranks + (col2[...] >> 1)
    entry = lax.broadcasted_iota(I32, (8, block), 0)
    place = lax.broadcasted_iota(I32, (tiles, block), 0).astype(F32).astype(BF16)
    slot = slot.astype(F32)
    one, nothing = jnp.ones((), BF16), jnp.zeros((), BF16)
    onehot, values = [], []
    for h in range(halves):
        same = jnp.broadcast_to(slot[h : h + 1].astype(BF16), (tiles, block)) == place
        onehot.append(jnp.where(same, one, nothing))
        row = jnp.broadcast_to(row2[h : h + 1], (8, block))
        device = jnp.where(row >= 0, row // ocean_blocks + 1, 0)
        local = jnp.where(row >= 0, row % ocean_blocks, 0)
        values.append(jnp.where(entry == 0, local, device).astype(F32).astype(BF16))
    found = lax.dot_general(
        jnp.concatenate(values, 1), jnp.concatenate(onehot, 1), ROWS_WITH_ROWS, preferred_element_type=F32
    )
    device = jnp.maximum(found[1:2, :ranks], found[1:2, ranks:])
    low_lanes = lax.broadcasted_iota(I32, (1, block), 1) < ranks // 2
    first, second = found[0:1, :ranks], found[0:1, ranks:]
    locals_of = (
        jnp.where(low_lanes, first, pltpu.roll(second, ranks // 2, 1)),
        jnp.where(low_lanes, pltpu.roll(first, ranks // 2, 1), second),
    )
    for h in range(2):
        info = jnp.concatenate([device, locals_of[h]], 0).astype(BF16)

        def tell(s, carry, info=info):
            out_ref[s * CHUNK + 2 * TILE_PAIRS] = info
            return carry

        lax.fori_loop(h * ranks // 2, (h + 1) * ranks // 2, tell, 0, unroll=16)

    def widen(g, carry):
        at = pl.ds(pl.multiple_of(g * 16, 16), 16)
        weight[at] = weight_in[at].astype(F32)
        return carry

    def pair_up(g, carry):
        base = pl.multiple_of(g * 32, 32)
        at = [pl.ds(base + k, 8, ENTRIES) for k in range(ENTRIES)]
        targets, weights = regroup([target_in[a, :] for a in at], [weight[a, :] for a in at])
        for k in range(ENTRIES):
            target[at[k], :] = targets[k].astype(F32)
            weight[at[k], :] = weights[k]
        return carry

    def send(t, carry):
        home = col[t]
        base = (home >> 1) * CHUNK + (home & 1) * TILE_PAIRS
        line = pl.multiple_of(t * ENTRIES, ENTRIES)
        for h in range(2):
            at = pl.ds(line + 2 * h, 2)
            out_ref[base + h] = weight[at, :].astype(BF16)
            out_ref[base + 2 + h] = target[at, :].astype(BF16)
        return carry

    def each(part, size, body, unroll):
        count = stage_lines // size
        lax.fori_loop(part * count, (part + 1) * count, body, 0, unroll=unroll)

    for i in range(STAGES):
        stages[i][0].wait()
        each(i, 16, widen, 16)
        stages[i][1].wait()
        each(i, 32, pair_up, 8)
        if i == 0:
            col_copy.wait()
        each(i, ENTRIES, send, stage_tiles)


def flux_kernel(
    owner_hbm, bits_hbm, atm_hbm, sent_hbm, out, slot_hbm,
    owner, slot, count, bits, atm, ocean, sems,
):
    blocks, fields, block = atm.shape
    words = bits.shape[0]
    copies = start_copies(((owner_hbm, owner), (bits_hbm, bits), (atm_hbm, atm)), sems)

    def clear(c, carry):
        count[c] = 0
        return carry

    lax.fori_loop(0, count.shape[0], clear, 0, unroll=16)
    copies[0].wait()

    def home(b, carry):
        to = owner[b]
        rank = count[to]
        count[to] = rank + 1
        slot[b] = 2 * to + rank
        return carry

    lax.fori_loop(0, blocks, home, 0, unroll=8)
    slots_out = pltpu.make_async_copy(slot, slot_hbm, sems.at[3])
    slots_out.start()

    copies[1].wait()
    column = lax.broadcasted_iota(I32, (blocks, block), 1)
    word = column // 30
    packed = jnp.concatenate([bits[...], jnp.zeros((8 - words, blocks), I32)], 0).T
    picked = jnp.zeros((blocks, block), I32)
    for w in range(words):
        picked = jnp.where(word == w, jnp.broadcast_to(packed[:, w : w + 1], (blocks, block)), picked)
    ocean[...] = jnp.right_shift(picked, column - word * 30) & 1

    copies[2].wait()
    field = lax.broadcasted_iota(I32, (8, block), 0)

    def fluxes_of(b):
        state = atm[b, 0:16, :].astype(F32)
        head = state[0:8]
        wind_east = head[0:1]
        wind_north = head[1:2]
        speed = jnp.sqrt(wind_east * wind_east + wind_north * wind_north + 0.25)
        drive = jnp.where(field < 2, head, pltpu.roll(head, 6, 0) - head)
        is_ocean = jnp.broadcast_to(ocean[pl.ds(b, 1), :], (8, block)) == 1
        head = jnp.where(is_ocean & (field < 4), (0.5 * speed) * drive, head)
        return jnp.concatenate([jnp.concatenate([head, state[8:16]], 0).astype(BF16), atm[b, 16:fields, :]], 0)

    def pair(p, carry):
        out[p] = jnp.concatenate([fluxes_of(2 * p), fluxes_of(2 * p + 1)], 0).T
        return carry

    lax.fori_loop(0, blocks // 2, pair, 0, unroll=4)
    slots_out.wait()


def remap_kernel(
    ranks, slot_hbm, recv, flux, out_ref, owner_ref,
    slot, sum_even, sum_odd, rows_vmem, rows, sems,
):
    pairs, block, _ = flux.shape
    fields = out_ref.shape[1]
    copies = start_copies(((slot_hbm, slot),), sems)
    me = lax.axis_index("comp") * lax.axis_size("cpl") + lax.axis_index("cpl")
    lane = lax.broadcasted_iota(I32, (2, block), 1)
    other = ranks // 2
    mine = lax.rem(me, other)

    def hear(c, carry):
        local0, local1 = carry
        info = recv[c * CHUNK + 2 * TILE_PAIRS].astype(F32)
        moved = pltpu.roll(info, lax.rem(c - mine + ranks, ranks), 1)
        local0 = jnp.maximum(local0, jnp.where(lane == c, moved, 0.0))
        local1 = jnp.maximum(local1, jnp.where(lane == (c ^ other), moved, 0.0))
        return local0, local1

    zeros = jnp.zeros((2, block), F32)
    local0, local1 = lax.fori_loop(0, ranks, hear, (zeros, zeros), unroll=ranks)
    padding = jnp.zeros((6, block), F32)
    rows_vmem[...] = jnp.concatenate([local0[1:2], local1[1:2], padding], 0).astype(I32)
    rows_in = pltpu.make_async_copy(rows_vmem, rows, sems.at[1])
    rows_in.start()

    def hear_device(c, device):
        return jnp.maximum(device, recv[c * CHUNK + 2 * TILE_PAIRS].astype(F32))

    device = lax.fori_loop(0, ranks, hear_device, zeros, unroll=ranks)
    owner_ref[...] = jnp.concatenate([device, padding], 0)
    sum_even[...] = jnp.zeros_like(sum_even)
    sum_odd[...] = jnp.zeros_like(sum_odd)
    column = lax.broadcasted_iota(I32, (block, block), 0).astype(F32).astype(BF16)
    nothing = jnp.zeros((), BF16)

    def spread(x):
        return jnp.broadcast_to(x, (block, block))

    def dense(b):
        home = slot[b]
        source = home >> 1
        rank = home & 1
        base = source * CHUNK + rank * TILE_PAIRS

        def two(h):
            weight = recv[base + h]
            target = recv[base + 2 + h]
            second = jnp.where(spread(target[1:2]) == column, spread(weight[1:2]), nothing)
            return jnp.where(spread(target[0:1]) == column, spread(weight[0:1]), second)

        return rows[rank, source ^ (rank * other)], jnp.concatenate([two(0), two(1)], 1)

    def pair(p, carry):
        row0, dense0 = dense(2 * p)
        row1, dense1 = dense(2 * p + 1)
        both = flux[p]
        terms = jnp.dot(
            jnp.concatenate([dense0, dense1], 0), jnp.concatenate([both, both], 0), preferred_element_type=F32
        )
        sum_even[row0] += terms[:block]
        sum_odd[row1] += terms[block:]
        return carry

    for copy in copies:
        copy.wait()
    rows_in.wait()
    lax.fori_loop(0, pairs, pair, 0, unroll=pairs)
    low_lanes = lax.broadcasted_iota(I32, (block, 2 * fields), 1) < fields
    for q in range(0, out_ref.shape[0], 2):
        total = jnp.where(low_lanes, sum_even[q], sum_odd[q + 1])
        total += pltpu.roll(jnp.where(low_lanes, sum_even[q + 1], sum_odd[q]), fields, 1)
        both = total.T
        out_ref[q] = both[:fields]
        out_ref[q + 1] = both[fields:]


def permute_kernel(owner_ref, x_ref, out_ref):
    ranks, pieces, block = x_ref.shape
    owner = owner_ref[0:1].astype(I32) - 1
    chosen = lax.broadcasted_iota(I32, (ranks, ranks), 0) == jnp.broadcast_to(owner, (ranks, ranks))
    chosen = chosen.astype(F32).astype(BF16)
    value = jnp.concatenate([x_ref[:, k, :] for k in range(pieces)], 1)
    high = value.astype(BF16)
    left = value - high.astype(F32)
    middle = left.astype(BF16)
    low = (left - middle.astype(F32)).astype(BF16)
    total = jnp.dot(
        jnp.concatenate([chosen] * 3, 1), jnp.concatenate([high, middle, low], 0), preferred_element_type=F32
    )
    for k in range(pieces):
        out_ref[:, k, :] = total[:, k * block : (k + 1) * block]


def hbm():
    return pl.BlockSpec(memory_space=pltpu.HBM)


def vmem():
    return pl.BlockSpec(memory_space=pltpu.VMEM)


def in_hbm(x):
    return pltpu.with_memory_space_constraint(x, pltpu.HBM)


def exchange(x):
    return lax.all_to_all(x, AXES, split_axis=0, concat_axis=0, tiled=True)


def on_device(atm_fields, land_bits, coupler_owner, tile_col, tile_row, tile_weight, tile_target):
    ranks = lax.axis_size("comp") * lax.axis_size("cpl")
    blocks, fields, block = atm_fields.shape
    words = land_bits.shape[1]
    tiles = tile_col.shape[0]
    lines = tiles * ENTRIES
    ocean_blocks = blocks // RATIO
    params = pltpu.CompilerParams(vmem_limit_bytes=VMEM_LIMIT)

    send = pl.pallas_call(
        lambda *refs: pack_kernel(ranks, ocean_blocks, *refs),
        out_shape=jax.ShapeDtypeStruct((ranks * CHUNK, 2, block), BF16),
        in_specs=[hbm()] * 5,
        out_specs=vmem(),
        scratch_shapes=[
            pltpu.SMEM((tiles,), I32),
            pltpu.VMEM((tiles // block, block), I32),
            pltpu.VMEM((tiles // block, block), I32),
            pltpu.VMEM((lines, block), BF16),
            pltpu.VMEM((lines, block), I32),
            pltpu.VMEM((lines, block), F32),
            pltpu.VMEM((lines, block), F32),
            pltpu.SemaphoreType.DMA((3 + 2 * STAGES,)),
        ],
        compiler_params=params,
        name="pack",
    )(
        in_hbm(tile_col),
        in_hbm(tile_col.reshape(tiles // block, block)),
        in_hbm(tile_row.reshape(tiles // block, block)),
        in_hbm(tile_weight.reshape(lines, block)),
        in_hbm(tile_target.reshape(lines, block)),
    )
    recv = exchange(send)

    fluxes, slot = pl.pallas_call(
        flux_kernel,
        out_shape=(pltpu.VMEM((blocks // 2, block, 2 * fields), BF16), pltpu.HBM((blocks,), I32)),
        in_specs=[hbm()] * 3 + [pl.BlockSpec(memory_space=pl.ANY)],
        out_specs=(vmem(), hbm()),
        scratch_shapes=[
            pltpu.SMEM((blocks,), I32),
            pltpu.SMEM((blocks,), I32),
            pltpu.SMEM((ranks,), I32),
            pltpu.VMEM((words, blocks), I32),
            pltpu.VMEM((blocks, fields, block), BF16),
            pltpu.VMEM((blocks, block), I32),
            pltpu.SemaphoreType.DMA((4,)),
        ],
        compiler_params=params,
        cost_estimate=pl.CostEstimate(flops=10_000_000, bytes_accessed=4_000_000, transcendentals=0),
        name="flux",
    )(in_hbm(coupler_owner), in_hbm(land_bits.T), in_hbm(atm_fields), send)

    sums, owner = pl.pallas_call(
        lambda *refs: remap_kernel(ranks, *refs),
        out_shape=(
            jax.ShapeDtypeStruct((ocean_blocks, fields, block), F32),
            jax.ShapeDtypeStruct((8, block), F32),
        ),
        in_specs=[hbm(), vmem(), vmem()],
        out_specs=(vmem(), vmem()),
        scratch_shapes=[
            pltpu.SMEM((blocks,), I32),
            pltpu.VMEM((ocean_blocks, block, 2 * fields), F32),
            pltpu.VMEM((ocean_blocks, block, 2 * fields), F32),
            pltpu.VMEM((8, block), I32),
            pltpu.SMEM((8, block), I32),
            pltpu.SemaphoreType.DMA((2,)),
        ],
        compiler_params=params,
        name="remap",
    )(in_hbm(slot), recv, fluxes)

    pieces = ocean_blocks * fields // ranks
    spread = exchange(sums.reshape(ranks, pieces, block))
    turned = pl.pallas_call(
        permute_kernel,
        out_shape=jax.ShapeDtypeStruct(spread.shape, F32),
        in_specs=[vmem(), vmem()],
        out_specs=vmem(),
        compiler_params=params,
        name="permute",
    )(owner, spread)
    return exchange(turned).reshape(ocean_blocks, fields, block)


def solution(mesh):
    in_specs = (
        P(AXES, None, None),
        P(AXES, None),
        P(AXES),
        P(AXES),
        P(AXES),
        P(AXES, None, None),
        P(AXES, None, None),
    )
    return jax.shard_map(
        on_device, mesh=mesh, in_specs=in_specs, out_specs=P(AXES, None, None), check_vma=False
    )
```
